32 devices in a mesh: section: 2 (over core), dp: 4 (over z), row: 2 (over x), col: 2 (over y).
Axes of the slice: x: 2, y: 2, z: 4, core: 2. Of those that a mesh axis runs over, the one named last changes fastest.
Arguments:
- tokens_in: bfloat16 [16, 256, 4, 512], P('dp', None, ('row', 'col')), may hold values from -6 to 6
- lengths: int32 [16], replicated, may hold values from 1 to 512, 5120 in all
- placement: int32 [16], replicated, may hold values from 0 to 15, each once
- cotangent: bfloat16 [16, 256, 4, 512], P('dp', None, ('row', 'col')), may hold values from -6 to 6
- qkv_weight: bfloat16 [2, 3, 1024, 1024], P('section', None, 'row', 'col'), may hold values from -0.1875 to 0.1875
- qv_bias: float32 [2, 2, 2, 2, 256], P('section', None, 'col', 'row'), may hold values from -3 to 3
- out_weight: bfloat16 [2, 1024, 1024], P('section', 'col', 'row'), may hold values from -0.375 to 0.375
- out_bias: float32 [2, 1024], P('section', ('row', 'col')), may hold values from -3 to 3
- norm1_gain: float32 [2, 1024], P('section', ('row', 'col')), may hold values from 0.5 to 1.5
- norm1_shift: float32 [2, 1024], P('section', ('row', 'col')), may hold values from -3 to 3
- up_weight: bfloat16 [2, 1024, 4096], P('section', 'row', 'col'), may hold values from -0.1875 to 0.1875
- up_bias: float32 [2, 2, 2, 1024], P('section', 'col', 'row'), may hold values from -3 to 3
- down_weight: bfloat16 [2, 4096, 1024], P('section', 'col', 'row'), may hold values from -0.09375 to 0.09375
- down_bias: float32 [2, 1024], P('section', ('row', 'col')), may hold values from -3 to 3
- norm2_gain: float32 [2, 1024], P('section', ('row', 'col')), may hold values from 0.5 to 1.5
- norm2_shift: float32 [2, 1024], P('section', ('row', 'col')), may hold values from -3 to 3
Outputs:
- layer_out: bfloat16 [2, 16, 256, 4, 512], P('section', 'dp', None, ('row', 'col'))
- input_grad: float32 [2, 16, 256, 4, 512], P('section', 'dp', None, ('row', 'col'))
- qkv_weight_grad: float32 [2, 3, 1024, 1024], P('section', None, 'row', 'col')
- qv_bias_grad: float32 [2, 2, 2, 2, 256], P('section', None, 'col', 'row')
- out_weight_grad: float32 [2, 1024, 1024], P('section', 'col', 'row')
- out_bias_grad: float32 [2, 1024], P('section', ('row', 'col'))
- norm1_gain_grad: float32 [2, 1024], P('section', ('row', 'col'))
- norm1_shift_grad: float32 [2, 1024], P('section', ('row', 'col'))
- up_weight_grad: float32 [2, 1024, 4096], P('section', 'row', 'col')
- up_bias_grad: float32 [2, 2, 2, 1024], P('section', 'col', 'row')
- down_weight_grad: float32 [2, 4096, 1024], P('section', 'col', 'row')
- down_bias_grad: float32 [2, 1024], P('section', ('row', 'col'))
- norm2_gain_grad: float32 [2, 1024], P('section', ('row', 'col'))
- norm2_shift_grad: float32 [2, 1024], P('section', ('row', 'col'))
The draws below stay inside these ranges and needn't reach their ends.
Inputs may be any that keep to these rules, and one draw needn't show every extreme that they name: `lengths`: the valid tokens of each sequence, at the start of its 512 slots; the other slots are padding. `placement`: names each sequence 0 to 15 exactly once.
All inputs are finite; a program needn't handle non-finite values.
Results may differ from the reference program's by a relative error of at most 0.014.
Values may be sent and summed in bfloat16 or wider, within the bound.
No kernel may reach another device: no remote copies, remote signals or barrier semaphores. Data moves between devices by JAX's collectives and lax.ppermute only.
A program may use at most 320 MiB of HBM per device.

```python
import math
import jax
import jax.numpy as jnp
import numpy as np
from jax import lax

D = 1024
HEADS = 16
HD = 64
FF = 4096
L = 512
SEQS = 16
SHARD_D = 256
SHARD_FF = 1024
N_ROW = 2
N_COL = 2


def level_of(rng, extent, cuts, least, high):
    loudness = 1.0
    for axis_at, parts in cuts:
        draws = jax.random.uniform(jax.random.fold_in(jax.random.fold_in(rng, 6), axis_at), (parts,), jnp.float32, least / len(cuts), high / len(cuts))
        loudness = loudness * jnp.repeat(jnp.exp(draws), extent[axis_at] // parts).reshape((-1,) + (1,) * (len(extent) - 1 - axis_at))
    return loudness


def split_up(count, total, most, lean):
    weights = [(1 << 20) // math.isqrt(rank ** lean) + 1 for rank in range(2, count + 1)]
    surplus, counts = total - most - (count - 1), [1] * (count - 1)
    while surplus > 0:
        movable = [i for i in range(count - 1) if counts[i] < most]
        whole, remaining = sum([weights[i] for i in movable]), surplus
        for i in movable:
            extra = min(most - counts[i], max(1, remaining * weights[i] // whole), surplus)
            counts[i] = counts[i] + extra
            surplus = surplus - extra
    return np.array([most] + counts)


def uneven_parts(stream_key, number_of, total, limit, slope):
    if number_of == 2:
        one = jax.random.randint(stream_key, (), max(1, total - limit), min(limit, total - 1) + 1)
        return jnp.stack([one, total - one])
    sizes = jnp.asarray(split_up(number_of, total, limit, slope), jnp.int32)
    couples = (number_of - 1) // 2
    source_of, receiver = sizes[1:1 + 2 * couples:2], sizes[2:2 + 2 * couples:2]
    room = jnp.minimum(source_of - 1, limit - receiver)
    shifted = jax.random.randint(jax.random.fold_in(stream_key, 1), (couples,), 0, 1 << 20) % (room + 1)
    sizes = sizes.at[1:1 + 2 * couples:2].set(source_of - shifted).at[2:2 + 2 * couples:2].set(receiver + shifted)
    return sizes[jax.random.permutation(jax.random.fold_in(stream_key, 2), number_of)]


def centred(rng, dims, width, bound, shards=(), held_as=jnp.bfloat16):
    drawn = jax.random.normal(rng, dims, jnp.float32) * width
    if len(shards) > 0:
        drawn = level_of(rng, dims, shards, -0.22, 0.18) * drawn
    return jnp.clip(drawn, min=-bound, max=bound).astype(held_as)


def setup_inputs(seed: int = 0) -> dict:
    key_list = jax.random.split(jax.random.key(seed), 17)
    return {
        "tokens_in": centred(key_list[0], (SEQS, L // 2, N_ROW * N_COL, 2 * SHARD_D), 1.0, 6.0, ((0, 4), (2, 4))),
        "lengths": uneven_parts(key_list[1], SEQS, SEQS * L * 5 // 8, L, 2).astype(jnp.int32),
        "placement": jax.random.permutation(key_list[2], SEQS).astype(jnp.int32),
        "cotangent": centred(key_list[3], (SEQS, L // 2, N_ROW * N_COL, 2 * SHARD_D), 1.0, 6.0, ((0, 4), (2, 4))),
        "qkv_weight": centred(key_list[4], (2, 3, D, D), D ** -0.5, 0.1875, ((0, 2), (2, 2), (3, 2))),
        "qv_bias": centred(key_list[5], (2, 2, N_COL, N_ROW, SHARD_D), 0.5, 3.0, ((0, 2), (2, 2), (3, 2)), jnp.float32),
        "out_weight": centred(key_list[6], (2, D, D), (D // 4) ** -0.5, 0.375, ((0, 2), (1, 2), (2, 2))),
        "out_bias": centred(key_list[7], (2, D), 0.5, 3.0, ((0, 2), (1, 4)), jnp.float32),
        "norm1_gain": jnp.clip(1.0 + 0.1 * jax.random.normal(key_list[8], (2, D), jnp.float32), 0.5, 1.5),
        "norm1_shift": centred(key_list[9], (2, D), 0.5, 3.0, ((0, 2), (1, 4)), jnp.float32),
        "up_weight": centred(key_list[10], (2, D, FF), D ** -0.5, 0.1875, ((0, 2), (1, 2), (2, 2))),
        "up_bias": centred(key_list[11], (2, N_COL, N_ROW, SHARD_FF), 0.5, 3.0, ((0, 2), (1, 2), (2, 2)), jnp.float32),
        "down_weight": centred(key_list[12], (2, FF, D), FF ** -0.5, 0.09375, ((0, 2), (1, 2), (2, 2))),
        "down_bias": centred(key_list[13], (2, D), 0.5, 3.0, ((0, 2), (1, 4)), jnp.float32),
        "norm2_gain": jnp.clip(1.0 + 0.1 * jax.random.normal(key_list[14], (2, D), jnp.float32), 0.5, 1.5),
        "norm2_shift": centred(key_list[15], (2, D), 0.5, 3.0, ((0, 2), (1, 4)), jnp.float32),
    }


EPSILON = 1e-05
MASKED = -1000000000.0

@jax.custom_vjp
def low(v):
    return lax.optimization_barrier(v.astype(jnp.bfloat16)).astype(jnp.float32)

@jax.custom_vjp
def low_back(v):
    return v

def low_keep(v):
    return (low(v), None)

def low_pass(kept, grad):
    return (grad,)

def back_keep(v):
    return (v, None)

def back_low(kept, grad):
    return (low(grad),)
low.defvjp(low_keep, low_pass)
low_back.defvjp(back_keep, back_low)

def matmul(left_side, right_side):
    return jnp.dot(left_side, right_side, precision=lax.Precision.HIGHEST, preferred_element_type=jnp.float32)

def to_rows(stored_rows):
    block_count = N_ROW * N_COL
    split = stored_rows.reshape(SEQS, L // 2, block_count, 2, SHARD_D)
    return split.transpose(0, 1, 3, 2, 4).reshape(SEQS * L, D)

def to_slots(token_rows):
    block_count = N_ROW * N_COL
    split = token_rows.reshape(SEQS, L // 2, 2, block_count, SHARD_D)
    return split.transpose(0, 1, 3, 2, 4).reshape(SEQS, L // 2, block_count, 2 * SHARD_D)

def layer_norm(values, norm_gain, norm_shift):
    center = lax.optimization_barrier(jnp.mean(values, axis=-1, keepdims=True))
    spread = values - center
    variance = lax.optimization_barrier(jnp.mean(spread * spread, axis=-1, keepdims=True))
    return spread * lax.rsqrt(variance + EPSILON) * norm_gain + norm_shift

def gelu_exact(values):
    return 0.5 * values * (1.0 + lax.erf(values * 2.0 ** (-0.5)))

def attend_sequence(pieces):
    queries, key_rows, value_rows, length = pieces
    product = jnp.einsum('qhd,khd->hqk', queries, key_rows, precision=lax.Precision.HIGHEST)
    scores = low_back(product * HD ** (-0.5))
    visible = jnp.arange(L, dtype=jnp.int32) < length
    scores = jnp.where(visible[None, None, :], scores, MASKED)
    highest = lax.optimization_barrier(jnp.max(scores, axis=-1, keepdims=True))
    weights_exp = jnp.exp(scores - highest)
    soft_weights = low(weights_exp / lax.optimization_barrier(jnp.sum(weights_exp, axis=-1, keepdims=True)))
    return jnp.einsum('hqk,khd->qhd', soft_weights, value_rows, precision=lax.Precision.HIGHEST)

def layer_apply(inputs, lengths, section_index, params):
    qkv_block, qv_block, out_block, out_shift, gain_one, shift_one, up_block, up_shift, down_block, down_shift, gain_two, shift_two = [tensor[section_index] for tensor in params]
    queries = low(low_back(matmul(inputs, qkv_block[0]) + qv_block[0].reshape(D)))
    key_rows = low(low_back(matmul(inputs, qkv_block[1])))
    values = low(low_back(matmul(inputs, qkv_block[2]) + qv_block[1].reshape(D)))
    layout = (SEQS, L, HEADS, HD)
    context = lax.map(jax.checkpoint(attend_sequence), (queries.reshape(layout), key_rows.reshape(layout), values.reshape(layout), lengths))
    context = low(low_back(context.reshape(SEQS * L, D)))
    attended = low_back(matmul(context, out_block) + out_shift)
    normed = layer_norm(inputs + attended, gain_one, shift_one)
    preact = low_back(matmul(low(normed), up_block) + up_shift.reshape(FF))
    active = low(gelu_exact(preact))
    branch = low_back(matmul(active, down_block) + down_shift)
    return layer_norm(normed + branch, gain_two, shift_two)

def reference(tokens_in, lengths, placement, cotangent, qkv_weight, qv_bias, out_weight, out_bias, norm1_gain, norm1_shift, up_weight, up_bias, down_weight, down_bias, norm2_gain, norm2_shift):
    params = tuple((tensor.astype(jnp.float32) for tensor in (qkv_weight, qv_bias, out_weight, out_bias, norm1_gain, norm1_shift, up_weight, up_bias, down_weight, down_bias, norm2_gain, norm2_shift)))
    order = placement.astype(jnp.int32)
    dealt_lengths = jnp.take(lengths, order)
    start_rows = to_rows(jnp.take(tokens_in, order, axis=0).astype(jnp.float32))

    def first_section(inputs, weights):
        return low(layer_apply(inputs, dealt_lengths, 0, weights))

    def second_section(inputs, weights):
        return layer_apply(inputs, dealt_lengths, 1, weights)
    middle, pull_first = jax.vjp(first_section, start_rows, params)
    final_rows, pull_second = jax.vjp(second_section, middle, params)
    grad_middle, grads_second = pull_second(to_rows(cotangent.astype(jnp.float32)))
    grad_start, grads_first = pull_first(grad_middle)
    totals = jax.tree.map(lambda first_part, second_part: first_part + second_part, grads_first, grads_second)
    layer_out = jnp.stack([to_slots(middle), to_slots(final_rows)]).astype(jnp.bfloat16)
    dealt_grad = jnp.stack([to_slots(grad_start), to_slots(grad_middle)])
    input_grad = jnp.zeros_like(dealt_grad).at[:, order].set(dealt_grad)
    return (layer_out, input_grad, totals[0], totals[1], totals[2], totals[3], totals[4], totals[5], totals[6], totals[7], totals[8], totals[9], totals[10], totals[11])
```

```python
import functools

import jax
import jax.numpy as jnp
from jax import lax
from jax.sharding import PartitionSpec as P

HD = 64
EPSILON = 1e-05
MASKED = -1000000000.0
F32 = jnp.float32
LOW = jnp.bfloat16


def dot(left, right):
    return lax.dot_general(left, right, (((1,), (0,)), ((), ())), preferred_element_type=F32)


def dot_nt(left, right):
    return lax.dot_general(left, right, (((1,), (1,)), ((), ())), preferred_element_type=F32)


def dot_tn(left, right):
    return lax.dot_general(left, right, (((0,), (0,)), ((), ())), preferred_element_type=F32)


def fetch(value, axis, steps):
    count = lax.axis_size(axis)
    return lax.ppermute(value, axis, [((place + steps) % count, place) for place in range(count)])


def send(value, axis, steps):
    count = lax.axis_size(axis)
    return lax.ppermute(value, axis, [(place, (place + steps) % count) for place in range(count)])


def swap_section(value):
    return lax.ppermute(value, "section", [(0, 1), (1, 0)])


def gather_blocks(piece, outer, inner):
    outer_count, inner_count = lax.axis_size(outer), lax.axis_size(inner)
    if outer_count == 2 and inner_count == 2:
        half = piece.shape[0] // 2
        far = fetch(piece, outer, 1)
        near = fetch(piece, inner, 1)
        top = fetch(far[:half], inner, 1)
        bottom = fetch(near[half:], outer, 1)
        return [[piece, near], [far, jnp.concatenate([top, bottom])]]
    blocks = []
    for out_steps in range(outer_count):
        own = piece if out_steps == 0 else fetch(piece, outer, out_steps)
        blocks.append([own if steps == 0 else fetch(own, inner, steps) for steps in range(inner_count)])
    return blocks


def add_low(left, right):
    return (left.astype(F32) + right.astype(F32)).astype(LOW)


def scatter_grad(rows, columns, row_axis, column_axis):
    row_count, column_count = len(rows), len(columns)
    if row_count == 2 and column_count == 2:
        half = rows[0].shape[1] // 2
        width = columns[0].shape[1]
        wide = jnp.concatenate(columns, axis=1)
        low_rows = jnp.concatenate([rows[0][:, half:], rows[1][:, half:]], axis=1)
        away = dot_tn(rows[1][:, :half], wide).astype(LOW)
        first = send(away, row_axis, 1)
        away = dot_tn(low_rows, columns[1]).astype(LOW)
        second = send(away, column_axis, 1)
        first = add_low(dot_tn(rows[0][:, :half], wide), first)
        second = add_low(dot_tn(low_rows, columns[0]), second)
        first_far = send(first[:, width:], column_axis, 1)
        second_far = send(second[half:], row_axis, 1)
        return jnp.concatenate([add_low(first[:, :width], first_far), add_low(second[:half], second_far)])
    total = dot_tn(rows[0], columns[0])
    for row_steps in range(row_count):
        for column_steps in range(column_count):
            if row_steps == 0 and column_steps == 0:
                continue
            block = dot_tn(rows[row_steps], columns[column_steps]).astype(LOW)
            if row_steps:
                block = send(block, row_axis, row_steps)
            if column_steps:
                block = send(block, column_axis, column_steps)
            total = total + block.astype(F32)
    return total.astype(LOW)


def pair_sum(value):
    return value + swap_section(value)


def layer_norm(values, gain, shift):
    center = jnp.mean(values, axis=1, keepdims=True)
    spread = values - center
    inverse = lax.rsqrt(jnp.mean(spread * spread, axis=1, keepdims=True) + EPSILON)
    normal = spread * inverse
    return normal * gain + shift, normal, inverse


def layer_norm_back(upstream, normal, inverse, gain):
    scaled = upstream * gain
    first = jnp.mean(scaled, axis=1, keepdims=True)
    second = jnp.mean(scaled * normal, axis=1, keepdims=True)
    result = inverse * (scaled - first - normal * second)
    return result, jnp.sum(upstream * normal, axis=0), jnp.sum(upstream, axis=0)


def gelu_parts(values):
    cdf = 0.5 * (1.0 + lax.erf(values * 2.0 ** (-0.5)))
    return cdf


def split_heads(values, seqs):
    tokens, width = values.shape
    return values.reshape(seqs, tokens // seqs, width // HD, HD)


def masked_scores(queries, keys, lengths):
    product = jnp.einsum("sqhd,skhd->shqk", queries, keys, preferred_element_type=F32)
    visible = lax.broadcasted_iota(jnp.int32, (lengths.shape[0], keys.shape[1]), 1) < lengths[:, None]
    return jnp.where(visible[:, None, None, :], product * HD ** (-0.5), MASKED)


def attend(queries, keys, values, lengths):
    seqs = lengths.shape[0]
    query, key, value = (split_heads(t, seqs) for t in (queries, keys, values))
    scores = masked_scores(query, key, lengths)
    highest = jnp.max(scores, axis=-1, keepdims=True)
    exponent = jnp.exp(scores - highest)
    total = jnp.sum(exponent, axis=-1, keepdims=True)
    soft_low = (exponent / total).astype(LOW)
    context = jnp.einsum("shqk,skhd->sqhd", soft_low, value, preferred_element_type=F32)
    return context.reshape(queries.shape).astype(LOW), highest, total


def attend_back(upstream, queries, keys, values, lengths, highest, total):
    seqs = lengths.shape[0]
    query, key, value, grad = (split_heads(t, seqs) for t in (queries, keys, values, upstream))
    soft = jnp.exp(masked_scores(query, key, lengths) - highest) / total
    grad_value = jnp.einsum("shqk,sqhd->skhd", soft.astype(LOW), grad, preferred_element_type=F32)
    grad_soft = jnp.einsum("sqhd,skhd->shqk", grad, value, preferred_element_type=F32)
    centered = jnp.sum(soft * grad_soft, axis=-1, keepdims=True)
    grad_scores = (soft * (grad_soft - centered)).astype(LOW)
    factor = HD ** (-0.5)
    grad_query = jnp.einsum("shqk,skhd->sqhd", grad_scores, key, preferred_element_type=F32) * factor
    grad_key = jnp.einsum("shqk,sqhd->skhd", grad_scores, query, preferred_element_type=F32) * factor
    return tuple(t.reshape(queries.shape).astype(LOW) for t in (grad_query, grad_key, grad_value))


def parts_of(values, count):
    return jnp.split(values, count, axis=1)


def apply_in(values, blocks):
    pieces = parts_of(values, len(blocks))
    return [
        functools.reduce(jnp.add, [dot(pieces[i], blocks[i][j]) for i in range(len(blocks))])
        for j in range(len(blocks[0]))
    ]


def apply_in_back(grads, blocks):
    return jnp.concatenate(
        [
            functools.reduce(jnp.add, [dot_nt(grads[j], row[j]) for j in range(len(row))])
            for row in blocks
        ],
        axis=1,
    )


def forward(inputs, lengths, weights, small):
    qkv, out, up, down = weights
    source = inputs.astype(F32)
    quarter = qkv[0][0].shape[1] // 3
    projected = apply_in(inputs, qkv)
    queries, keys, values = (
        jnp.concatenate([block[:, n * quarter : (n + 1) * quarter] for block in projected], axis=1)
        for n in range(3)
    )
    queries = (queries + small["query_bias"]).astype(LOW)
    keys = keys.astype(LOW)
    values = (values + small["value_bias"]).astype(LOW)
    context, highest, total = attend(queries, keys, values, lengths)
    attended = pair_sum(jnp.concatenate(apply_in(context, out), axis=1))
    normed, normal_one, inverse_one = layer_norm(
        source + (attended + small["out_bias"]), small["norm1_gain"], small["norm1_shift"]
    )
    normed_low = normed.astype(LOW)
    preact = jnp.concatenate(apply_in(normed_low, up), axis=1) + small["up_bias"]
    active = (preact * gelu_parts(preact)).astype(LOW)
    branch = pair_sum(jnp.concatenate(apply_in(active, down), axis=1))
    output, normal_two, inverse_two = layer_norm(
        normed + (branch + small["down_bias"]), small["norm2_gain"], small["norm2_shift"]
    )
    kept = (
        inputs, queries, keys, values, highest, total, context, normal_one, inverse_one,
        normed_low, preact, active, normal_two, inverse_two,
    )
    return output, kept


def backward(upstream, lengths, weights, small, kept):
    qkv, out, up, down = weights
    (
        inputs, queries, keys, values, highest, total, context, normal_one, inverse_one,
        normed_low, preact, active, normal_two, inverse_two,
    ) = kept
    rows, columns = len(qkv), len(qkv[0])
    grads = {}
    grad_two, grads["norm2_gain"], grads["norm2_shift"] = layer_norm_back(
        upstream, normal_two, inverse_two, small["norm2_gain"]
    )
    branch_low = grad_two.astype(LOW)
    grads["down_bias"] = jnp.sum(branch_low.astype(F32), axis=0)
    branch_parts = parts_of(branch_low, rows)
    grad_active = apply_in_back(branch_parts, down)
    cdf = gelu_parts(preact)
    density = jnp.exp(-0.5 * preact * preact) * (2.0 * jnp.pi) ** (-0.5)
    preact_low = (grad_active * (cdf + preact * density)).astype(LOW)
    grads["up_bias"] = jnp.sum(preact_low.astype(F32), axis=0)
    preact_parts = parts_of(preact_low, columns)
    grad_normed = grad_two + pair_sum(apply_in_back(preact_parts, up))
    down_grad = scatter_grad(parts_of(active, columns), branch_parts, "col", "row")
    up_grad = scatter_grad(parts_of(normed_low, rows), preact_parts, "row", "col")
    grad_one, grads["norm1_gain"], grads["norm1_shift"] = layer_norm_back(
        grad_normed, normal_one, inverse_one, small["norm1_gain"]
    )
    attended_low = grad_one.astype(LOW)
    grads["out_bias"] = jnp.sum(attended_low.astype(F32), axis=0)
    attended_parts = parts_of(attended_low, rows)
    grad_context = apply_in_back(attended_parts, out).astype(LOW)
    out_grad = scatter_grad(parts_of(context, columns), attended_parts, "col", "row")
    grad_query, grad_key, grad_value = attend_back(
        grad_context, queries, keys, values, lengths, highest, total
    )
    grads["query_bias"] = jnp.sum(grad_query.astype(F32), axis=0)
    grads["value_bias"] = jnp.sum(grad_value.astype(F32), axis=0)
    packed = [
        jnp.concatenate(trio, axis=1)
        for trio in zip(*(parts_of(t, columns) for t in (grad_query, grad_key, grad_value)))
    ]
    grad_input = grad_one + pair_sum(apply_in_back(packed, qkv))
    qkv_grad = scatter_grad(parts_of(inputs, rows), packed, "row", "col")
    return grad_input, grads, (qkv_grad, out_grad, up_grad, down_grad)


HALVED = ("query_bias", "value_bias", "up_bias")
WHOLE = ("out_bias", "norm1_gain", "norm1_shift", "down_bias", "norm2_gain", "norm2_shift")


def body(
    tokens_in,
    lengths,
    placement,
    cotangent,
    qkv_weight,
    qv_bias,
    out_weight,
    out_bias,
    norm1_gain,
    norm1_shift,
    up_weight,
    up_bias,
    down_weight,
    down_bias,
    norm2_gain,
    norm2_shift,
):
    row_count, col_count = lax.axis_size("row"), lax.axis_size("col")
    grid = row_count * col_count
    section, group = lax.axis_index("section"), lax.axis_index("dp")
    row, col = lax.axis_index("row"), lax.axis_index("col")
    is_first = section == 0
    seq_local, half_slots, _, packed_width = tokens_in.shape
    features = packed_width // 2
    seq_total = placement.shape[0]
    seq_own = seq_local // grid
    tokens = seq_own * half_slots * 2
    width = features * grid

    def to_rows(stored):
        blocks = lax.all_to_all(stored, ("row", "col"), split_axis=0, concat_axis=2, tiled=True)
        blocks = blocks.reshape(seq_own, half_slots, row_count, col_count, 2, features)
        blocks = jnp.roll(blocks.transpose(0, 1, 4, 2, 3, 5), -row, axis=3)
        return blocks.reshape(tokens, width)

    def to_slots(rows_held):
        blocks = rows_held.reshape(seq_own, half_slots, 2, row_count, col_count, features)
        blocks = jnp.roll(blocks, row, axis=3).transpose(0, 1, 3, 4, 2, 5)
        blocks = blocks.reshape(seq_own, half_slots, grid, packed_width)
        return lax.all_to_all(blocks, ("row", "col"), split_axis=2, concat_axis=0, tiled=True)

    def both_layers(block, axis):
        half_one, half_two = jnp.split(block, 2, axis=axis)
        stays = jnp.where(is_first, half_one, half_two)
        came = swap_section(jnp.where(is_first, half_two, half_one))
        return jnp.where(is_first, stays, came), jnp.where(is_first, came, stays)

    qkv_block = qkv_weight[0].transpose(1, 0, 2)
    qkv_rows, _, qkv_width = qkv_block.shape
    qkv_halves = both_layers(qkv_block, 2)
    out_halves = both_layers(out_weight[0], 0)
    up_halves = both_layers(up_weight[0], 1)
    down_halves = both_layers(down_weight[0], 0)

    def transposed(blocks):
        return [list(line) for line in zip(*blocks)]

    weights = []
    for layer in range(2):
        weights.append(
            (
                gather_blocks(qkv_halves[layer].reshape(qkv_rows, -1), "row", "col"),
                transposed(gather_blocks(out_halves[layer], "row", "col")),
                gather_blocks(up_halves[layer], "row", "col"),
                transposed(gather_blocks(down_halves[layer], "row", "col")),
            )
        )

    small_own = (qv_bias, up_bias, out_bias, norm1_gain, norm1_shift, down_bias, norm2_gain, norm2_shift)
    sizes = [t.size for t in small_own]
    flat = jnp.concatenate([t.reshape(-1) for t in small_own])
    flat_all = lax.all_gather(flat, ("section", "row", "col"), axis=0).reshape(2, row_count, col_count, -1)
    starts = [sum(sizes[:n]) for n in range(len(sizes) + 1)]
    fields = [flat_all[..., starts[n] : starts[n + 1]] for n in range(len(sizes))]

    def own_half(by_col):
        halves = by_col.reshape(*by_col.shape[:-1], 2, -1)
        chosen = lax.dynamic_index_in_dim(halves, section, axis=halves.ndim - 2, keepdims=False)
        return jnp.roll(chosen, -col, axis=-2)

    smalls = []
    for layer in range(2):
        qv = fields[0][layer].reshape(row_count, col_count, 2, -1).transpose(2, 1, 0, 3)
        qv = own_half(qv.reshape(2, col_count, -1)).reshape(2, -1)
        up_shift = fields[1][layer].transpose(1, 0, 2).reshape(col_count, -1)
        small = {"query_bias": qv[0], "value_bias": qv[1], "up_bias": own_half(up_shift).reshape(-1)}
        for name, field in zip(WHOLE, fields[2:]):
            small[name] = jnp.roll(field[layer], -row, axis=0).reshape(-1)
        smalls.append(small)

    own_first = group * seq_local + (row * col_count + col) * seq_own
    own_lengths = lax.dynamic_slice_in_dim(lengths, own_first, seq_own)
    inputs = to_rows(tokens_in)

    cot_all = lax.all_gather(cotangent, "dp", axis=0, tiled=True)
    wanted = group * seq_local + lax.broadcasted_iota(jnp.int32, (seq_local,), 0)
    matches = placement[None, :] == wanted[:, None]
    position = jnp.sum(
        jnp.where(matches, lax.broadcasted_iota(jnp.int32, (seq_local, seq_total), 1), 0), axis=1
    )
    upstream = to_rows(jnp.take(cot_all, position, axis=0)).astype(F32)

    first_out, first_kept = forward(inputs, own_lengths, weights[0], smalls[0])
    first_low = first_out.astype(LOW)
    second_out, second_kept = forward(first_low, own_lengths, weights[1], smalls[1])

    own_out = to_slots(jnp.where(is_first, first_low, second_out.astype(LOW)))
    out_all = lax.all_gather(own_out, "dp", axis=0, tiled=True)
    chosen = lax.dynamic_slice_in_dim(placement, group * seq_local, seq_local)

    def small_sum(grads):
        parts = [jnp.roll(grads[name].reshape(col_count, -1), col, axis=0).reshape(-1) for name in HALVED]
        parts += [jnp.roll(grads[name].reshape(row_count, -1), row, axis=0).reshape(-1) for name in WHOLE]
        vector = jnp.concatenate(parts).reshape(-1, 128)
        for axis, count in (("row", row_count), ("col", col_count)):
            if count == 2:
                vector = vector + fetch(vector, axis, 1)
            else:
                vector = lax.psum(vector, axis)
        return vector.astype(LOW)

    grad_second, small_second, heavy_second = backward(
        upstream, own_lengths, weights[1], smalls[1], second_kept
    )
    heavy_second = lax.psum((*heavy_second, small_sum(small_second)), "dp")
    grad_second, out_all = lax.optimization_barrier((grad_second, out_all))
    layer_out = jnp.take(out_all, chosen, axis=0)
    grad_first, small_first, heavy_first = backward(
        grad_second, own_lengths, weights[0], smalls[0], first_kept
    )
    hidden_first, heavy_second = lax.optimization_barrier((heavy_first[2:], heavy_second))
    hidden_first = lax.psum(hidden_first, "dp")
    outer_first, hidden_first = lax.optimization_barrier(
        ((*heavy_first[:2], small_sum(small_first)), hidden_first)
    )
    outer_first = lax.psum(outer_first, "dp")
    heavy_first = (*outer_first[:2], *hidden_first, outer_first[2])
    input_grad = to_slots(jnp.where(is_first, grad_first, grad_second))

    def to_section(first, second, axis):
        stays = jnp.where(is_first, first, second)
        came = swap_section(jnp.where(is_first, second, first))
        halves = [jnp.where(is_first, stays, came), jnp.where(is_first, came, stays)]
        return jnp.concatenate(halves, axis=axis).astype(F32)

    def qkv_shape(value):
        return value.reshape(qkv_rows, 3, -1)

    qkv_grad = to_section(qkv_shape(heavy_first[0]), qkv_shape(heavy_second[0]), 2).transpose(1, 0, 2)
    out_grad = to_section(heavy_first[1], heavy_second[1], 0)
    up_grad = to_section(heavy_first[2], heavy_second[2], 1)
    down_grad = to_section(heavy_first[3], heavy_second[3], 0)
    small_halves = to_section(heavy_first[4].reshape(1, -1), heavy_second[4].reshape(1, -1), 0)
    model, hidden = width // 2, up_bias.size * grid // 2
    ends = (0, model, 2 * model, 2 * model + hidden)

    def own_col_row(begin, end):
        blocks = small_halves[:, begin:end].reshape(2, col_count, -1).transpose(1, 0, 2)
        blocks = blocks.reshape(col_count * row_count, -1)
        return lax.dynamic_index_in_dim(blocks, col * row_count + row, axis=0, keepdims=False)

    query_sum, value_sum, up_sum = (own_col_row(ends[n], ends[n + 1]) for n in range(3))
    qv_grad = jnp.stack([query_sum, value_sum]).reshape(qv_bias.shape)
    up_bias_grad = up_sum.reshape(up_bias.shape)
    rest = small_halves[0, ends[3] :].reshape(len(WHOLE), grid, features)
    rest = lax.dynamic_index_in_dim(rest, row * col_count + col, axis=1, keepdims=False)
    whole_grads = {name: rest[n][None] for n, name in enumerate(WHOLE)}
    return (
        layer_out[None],
        input_grad[None],
        qkv_grad[None],
        qv_grad,
        out_grad[None],
        whole_grads["out_bias"],
        whole_grads["norm1_gain"],
        whole_grads["norm1_shift"],
        up_grad[None],
        up_bias_grad,
        down_grad[None],
        whole_grads["down_bias"],
        whole_grads["norm2_gain"],
        whole_grads["norm2_shift"],
    )


def solution(mesh):
    tokens = P("dp", None, ("row", "col"), None)
    feature = P("section", ("row", "col"))
    outward = P("section", "col", "row")
    hidden = P("section", "col", "row", None)
    qv = P("section", None, "col", "row", None)
    stored = P("section", "dp", None, ("row", "col"), None)
    inward = P("section", "row", "col")
    qkv = P("section", None, "row", "col")
    params = (
        qkv, qv, outward, feature, feature, feature, inward, hidden, outward, feature, feature, feature,
    )
    return jax.shard_map(
        body,
        mesh=mesh,
        in_specs=(tokens, P(), P(), tokens, *params),
        out_specs=(stored, stored, *params),
        check_vma=False,
    )
```

```python
import functools
from typing import NamedTuple

import jax
import jax.numpy as jnp
from jax import lax
from jax.experimental import pallas as pl
from jax.experimental.pallas import tpu as pltpu
from jax.sharding import PartitionSpec as P

HD = 64
PAIR = 2 * HD
EPSILON = 1e-05
MASKED = -1000000000.0
F32 = jnp.float32
LOW = jnp.bfloat16
COST = 0.02
VMEM_LIMIT = 56 * 1024 * 1024
TILE = 256
NORM_TILE = 64


def dot(left, right):
    return lax.dot_general(left, right, (((1,), (0,)), ((), ())), preferred_element_type=F32)


def dot_nt(left, right):
    return lax.dot_general(left, right, (((1,), (1,)), ((), ())), preferred_element_type=F32)


def shaped(shape, dtype):
    return jax.ShapeDtypeStruct(shape, dtype)


def fetch(value, axis, steps):
    count = lax.axis_size(axis)
    return lax.ppermute(value, axis, [((place + steps) % count, place) for place in range(count)])


def send(value, axis, steps):
    count = lax.axis_size(axis)
    return lax.ppermute(value, axis, [(place, (place + steps) % count) for place in range(count)])


def swap_section(value):
    return lax.ppermute(value, "section", [(0, 1), (1, 0)])


def after(value, *others):
    return lax.optimization_barrier((value, others))[0]


def small_grid():
    return lax.axis_size("row") == 2 and lax.axis_size("col") == 2


def gather_rows(piece):
    return [[[piece]]] + [[[fetch(piece, "row", i)]] for i in range(1, lax.axis_size("row"))]


def gather_first(piece):
    if small_grid():
        return fetch(piece, "row", 1), fetch(piece, "col", 1)
    blocks = []
    for i in range(lax.axis_size("row")):
        own = piece if i == 0 else fetch(piece, "row", i)
        blocks.append([[own if j == 0 else fetch(own, "col", j)] for j in range(lax.axis_size("col"))])
    return blocks


def gather_second(piece, first, axis):
    if not small_grid():
        return first
    far, near = first
    corner = fetch(far, "col", 1) if axis == "col" else fetch(near, "row", 1)
    return [[[piece], [near]], [[far], [corner]]]


def gather_blocks(piece):
    return gather_second(piece, gather_first(piece), "col")


def add_low(left, right):
    return (left.astype(F32) + right.astype(F32)).astype(LOW)


def rows_sent(parts):
    return [send(parts[i], "row", i) for i in range(1, len(parts))]


def rows_sum(parts, came, half):
    return add_up([part[half].astype(F32) for part in (parts[0], *came)]).astype(LOW)


def scatter_first(parts, axis):
    return send(parts[1], axis, 1) if small_grid() else ()


def scatter_middle(parts, first):
    return [add_low(parts[0][n], first[n]) for n in range(2)] if small_grid() else ()


def scatter_second(middle, axis):
    return send(middle[1], "row" if axis == "col" else "col", 1) if small_grid() else ()


def scatter_last(parts, middle, second):
    if small_grid():
        return add_low(middle[0], second)
    (blocks,) = parts
    total = blocks[0, 0].astype(F32)
    for i in range(lax.axis_size("row")):
        for j in range(lax.axis_size("col")):
            if i or j:
                block = blocks[i, j]
                block = send(block, "row", i) if i else block
                block = send(block, "col", j) if j else block
                total = total + block.astype(F32)
    return total.astype(LOW)


def group_in(value):
    return lax.ppermute(value, "dp", [(0, 1), (3, 2)])


def group_across(value):
    return lax.ppermute(value, "dp", [(1, 2), (2, 1)])


def group_out(value):
    return lax.ppermute(value, "dp", [(1, 0), (2, 3)])


def pair_col(value):
    return lax.ppermute(value, "col", [(0, 1), (1, 0)])


def both_halves(got, *beside):
    got = after(got, *beside)
    return got, swap_section(got)


def to_pair(mine, others):
    return pair_col(add_low(mine, swap_section(others)))


class Slab(NamedTuple):
    name: str
    number: int
    start: int
    height: int


class Layout(NamedTuple):
    width: int
    slabs: tuple

    @property
    def height(self):
        return self.slabs[-1].start + self.slabs[-1].height

    def named(self, name):
        return [slab for slab in self.slabs if slab.name == name]


def make_layout(weights):
    width = min(columns for _, _, columns in weights)
    slabs, start = [], 0
    for name, rows, columns in weights:
        for number in range(columns // width):
            slabs.append(Slab(name, number, start, rows))
            start += rows
    return Layout(width, tuple(slabs))


def take_slab(pieces, slab):
    each = min(piece.shape[0] for piece in pieces)
    start = slab.start % each
    return pieces[slab.start // each][start : start + slab.height, :]


def add_up(terms):
    return functools.reduce(jnp.add, terms)


def times_rows(left, blocks, j, slab):
    height = slab.height
    return add_up(
        [dot(left[:, i * height : (i + 1) * height], take_slab(blocks[i][j], slab)) for i in range(len(blocks))]
    )


def times_columns(left, blocks, i, slab):
    height = slab.height
    return add_up(
        [dot(left[:, j * height : (j + 1) * height], take_slab(blocks[i][j], slab)) for j in range(len(blocks[i]))]
    )


def launch(kernel, outputs, operands, scratch=(), flops=0, scalars=()):
    leaves, tree = jax.tree.flatten(operands)
    count_in, count_scalar = len(leaves), len(scalars)

    def inner(*refs):
        ins = jax.tree.unflatten(tree, refs[count_scalar : count_scalar + count_in])
        kernel(refs[:count_scalar], ins, *refs[count_scalar + count_in :])

    moved = sum(t.size * t.dtype.itemsize for t in (*leaves, *outputs))
    return pl.pallas_call(
        inner,
        out_shape=tuple(outputs),
        in_specs=[pl.BlockSpec(memory_space=pltpu.SMEM)] * count_scalar
        + [pl.BlockSpec(memory_space=pltpu.VMEM)] * count_in,
        out_specs=tuple(pl.BlockSpec(memory_space=pltpu.VMEM) for _ in outputs),
        scratch_shapes=list(scratch),
        compiler_params=pltpu.CompilerParams(vmem_limit_bytes=VMEM_LIMIT),
        cost_estimate=pl.CostEstimate(flops=int(COST * flops), bytes_accessed=int(COST * moved), transcendentals=0),
    )(*scalars, *leaves)


def each_tile(count, size, step):
    def visit(number, carry):
        step(pl.ds(pl.multiple_of(number * size, size), size))
        return carry

    lax.fori_loop(0, count // size, visit, 0)


def stored_places(blocks, row):
    count, _, packed = blocks.shape
    features = packed // 2
    row_count = lax.axis_size("row")
    col_count = count // row_count
    for i in range(row_count):
        turned = lax.rem(row + i, row_count)
        for j in range(col_count):
            place = (i * col_count + j) * features
            yield turned * col_count + j, slice(place, place + features)


def unpack(blocks, row, target):
    half, packed = blocks.shape[1:]
    for block, lanes in stored_places(blocks, row):
        target[:half, lanes] = blocks[block, :, : packed // 2]
        target[half:, lanes] = blocks[block, :, packed // 2 :]


def pack(source, row, blocks):
    half, packed = blocks.shape[1:]
    for block, lanes in stored_places(blocks, row):
        blocks[block, :, : packed // 2] = source[:half, lanes]
        blocks[block, :, packed // 2 :] = source[half:, lanes]


def normalize(values):
    center = jnp.mean(values, axis=1, keepdims=True)
    spread = values - center
    inverse = lax.rsqrt(jnp.mean(spread * spread, axis=1, keepdims=True) + EPSILON)
    return spread * inverse, inverse


def head_mask(shape, head):
    lane = lax.broadcasted_iota(jnp.int32, shape, 1)
    return (lane >= head * HD) & (lane < (head + 1) * HD)


def both_heads(values):
    return [jnp.where(head_mask(values.shape, h), values, jnp.zeros_like(values)) for h in range(2)]


def halves_kernel(layout, sources, scalars, ins, keep_ref, send_ref):
    section = scalars[0][0]
    for place, target in ((section, keep_ref), (1 - section, send_ref)):
        for slab in layout.slabs:
            rows = slice(slab.start, slab.start + slab.height)
            source, by_rows = sources[slab.name]
            lanes = slice(slab.number * layout.width, (slab.number + 1) * layout.width)
            if by_rows:
                start = pl.multiple_of(place * slab.height, slab.height)
                target[rows, :] = source(ins)[pl.ds(start, slab.height), lanes]
            else:
                total = len(layout.named(slab.name)) * layout.width
                start = pl.multiple_of(place * total + slab.number * layout.width, layout.width)
                target[rows, :] = source(ins)[:, pl.ds(start, layout.width)]


def whole_kernel(layout, targets, scalars, ins, *refs):
    section = scalars[0][0]
    for place, source in ((section, ins[0]), (1 - section, ins[1])):
        for slab in layout.slabs:
            value = take_slab(source, slab).astype(F32)
            target, by_rows = targets[slab.name]
            lanes = slice(slab.number * layout.width, (slab.number + 1) * layout.width)
            if by_rows:
                start = pl.multiple_of(place * slab.height, slab.height)
                target(refs)[pl.ds(start, slab.height), lanes] = value
            else:
                total = len(layout.named(slab.name)) * layout.width
                start = pl.multiple_of(place * total + slab.number * layout.width, layout.width)
                target(refs)[:, pl.ds(start, layout.width)] = value


def attend_kernel(layout, scalars, ins, *refs):
    lengths, place = scalars
    source, query_bias, value_bias, blocks = ins
    if source.ndim == 3:
        tokens_ref, *refs = refs
        unpack(source, place[0], tokens_ref)
        source = tokens_ref
    query_ref, key_ref, value_ref, probs_ref, context_ref, part_ref = refs
    slots = source.shape[0]
    columns = len(blocks[0])
    half = query_ref.shape[1]
    biases = {"query": query_bias, "key": None, "value": value_bias}
    targets = {"query": query_ref, "key": key_ref, "value": value_ref}

    def project(rows):
        held = source[rows, :]
        for j in range(columns):
            for name, target in targets.items():
                for slab in layout.named(name):
                    start = j * (half // columns) + slab.number * layout.width
                    span = slice(start, start + layout.width)
                    result = times_rows(held, blocks, j, slab)
                    if biases[name] is not None:
                        result = result + biases[name][:, span]
                    target[rows, span] = result.astype(LOW)

    each_tile(slots, TILE, project)
    length = lengths[0]

    def heads(pair, carry):
        lanes = pl.ds(pl.multiple_of(pair * PAIR, PAIR), PAIR)
        keys = key_ref[:, lanes]
        values = both_heads(value_ref[:, lanes])
        for start in range(0, slots, TILE):
            rows = slice(start, start + TILE)
            terms = []
            for h, queries in enumerate(both_heads(query_ref[rows, lanes])):
                scores = dot_nt(queries, keys) * HD ** (-0.5)
                token = lax.broadcasted_iota(jnp.int32, (1, slots), 1)
                slot = jnp.where(token < slots // 2, 2 * token, 2 * token - (slots - 1))
                scores = jnp.where(slot < length, scores, MASKED)
                exponent = jnp.exp(scores - jnp.max(scores, axis=1, keepdims=True))
                probs = (exponent / jnp.sum(exponent, axis=1, keepdims=True)).astype(LOW)
                probs_ref[2 * pair + h, rows, :] = probs
                terms.append(dot(probs, values[h]))
            context_ref[rows, lanes] = add_up(terms).astype(LOW)
        return carry

    lax.fori_loop(0, half // PAIR, heads, 0)

    def project_out(rows):
        held = context_ref[rows, :]
        slabs = layout.named("out")
        for i in range(len(blocks)):
            for slab in slabs:
                start = (i * len(slabs) + slab.number) * layout.width
                part_ref[rows, start : start + layout.width] = times_columns(held, blocks, i, slab).astype(LOW)

    each_tile(slots, TILE, project_out)


def keep_half(source, section, target):
    height = target.shape[0]
    target[...] = source[pl.ds(pl.multiple_of(section * height, height), height), :]


def norm_kernel(scalars, ins, normed_ref, low_ref, half_ref, normal_ref, inverse_ref):
    source, own, came, out_bias, gain, shift = ins
    tokens = source.shape[0]

    def norm(rows):
        attended = own[rows, :].astype(F32) + came[rows, :].astype(F32)
        normal, inverse = normalize(source[rows, :].astype(F32) + (attended + out_bias[...]))
        normed = normal * gain[...] + shift[...]
        normed_ref[rows, :] = normed
        low_ref[rows, :] = normed.astype(LOW)
        normal_ref[rows, :] = normal.astype(LOW)
        inverse_ref[rows, :] = inverse

    each_tile(tokens, NORM_TILE, norm)
    keep_half(low_ref, scalars[0][0], half_ref)


def feed_kernel(layout, scalars, ins, active_ref, slope_ref, *part_refs):
    sources, up_bias, blocks = ins
    ups, downs = layout.named("up"), layout.named("down")
    first = 0
    for source, part_ref in zip(sources, part_refs):
        count = source.shape[0]

        def widen(rows, source=source, first=first):
            held = source[rows, :]
            here = pl.ds(first + rows.start, rows.size)
            for j in range(len(blocks[0])):
                for slab in ups:
                    start = (j * len(ups) + slab.number) * layout.width
                    span = slice(start, start + layout.width)
                    preact = times_rows(held, blocks, j, slab) + up_bias[:, span]
                    cdf = 0.5 * (1.0 + lax.erf(preact * 2.0 ** (-0.5)))
                    density = jnp.exp(-0.5 * preact * preact) * (2.0 * jnp.pi) ** (-0.5)
                    active_ref[here, span] = (preact * cdf).astype(LOW)
                    slope_ref[here, span] = (cdf + preact * density).astype(LOW)

        each_tile(count, TILE, widen)

        def narrow(rows, first=first, part_ref=part_ref):
            held = active_ref[pl.ds(first + rows.start, rows.size), :]
            for i in range(len(blocks)):
                for slab in downs:
                    start = (i * len(downs) + slab.number) * layout.width
                    part_ref[rows, start : start + layout.width] = times_columns(held, blocks, i, slab).astype(LOW)

        each_tile(count, TILE, narrow)
        first += count


def branch_tile(rows, own, came, mine, others, section):
    total = own[rows, :].astype(F32) + came[rows, :].astype(F32)
    height = mine.shape[0]
    inner = pl.ds(lax.rem(rows.start, height), rows.size)
    in_mine = rows.start // height == section
    pair = jnp.where(in_mine, mine[inner, :].astype(F32), others[inner, :].astype(F32))
    return total + pair


def finish_kernel(scalars, ins, output_ref, stored_ref, normal_ref, inverse_ref):
    section, place = scalars
    normed, own, came, mine, others, bias, gain, shift = ins

    def norm(rows):
        branch = branch_tile(rows, own, came, mine, others, section[0])
        normal, inverse = normalize(normed[rows, :] + (branch + bias[...]))
        output_ref[rows, :] = (normal * gain[...] + shift[...]).astype(LOW)
        normal_ref[rows, :] = normal.astype(LOW)
        inverse_ref[rows, :] = inverse

    each_tile(normed.shape[0], NORM_TILE, norm)
    half, packed = stored_ref.shape[1:]
    first = pl.ds(pl.multiple_of(section[0] * half, half), half)
    second = pl.ds(pl.multiple_of(2 * half + section[0] * half, half), half)
    for block, lanes in stored_places(stored_ref, place[0]):
        stored_ref[block, :, : packed // 2] = output_ref[first, lanes]
        stored_ref[block, :, packed // 2 :] = output_ref[second, lanes]


def norm_back(upstream, normal, inverse, gain):
    scaled = upstream * gain
    first = jnp.mean(scaled, axis=1, keepdims=True)
    second = jnp.mean(scaled * normal, axis=1, keepdims=True)
    return inverse * (scaled - first - normal * second)


def norm_back_tiles(given_of, normal, inverse, gain, grad_ref, low_ref, sums_ref):
    sums_ref[...] = jnp.zeros_like(sums_ref)

    def step(rows):
        given = given_of(rows)
        held = normal[rows, :].astype(F32)
        grad = norm_back(given, held, inverse[rows, :], gain[...])
        low = grad.astype(LOW)
        grad_ref[rows, :] = grad
        low_ref[rows, :] = low
        sums_ref[0:1, :] += jnp.sum(given * held, axis=0, keepdims=True)
        sums_ref[1:2, :] += jnp.sum(given, axis=0, keepdims=True)
        sums_ref[2:3, :] += jnp.sum(low.astype(F32), axis=0, keepdims=True)

    each_tile(normal.shape[0], NORM_TILE, step)


def norm_two_back_kernel(scalars, ins, *refs):
    section, place = scalars
    upstream, normal, inverse, gain = ins
    if len(upstream) > 1:
        given_ref, *refs = refs
    else:
        *refs, tokens_ref = refs
        unpack(upstream[0], place[0], tokens_ref)
    grad_ref, low_ref, half_ref, sums_ref = refs

    def given_of(rows):
        if len(upstream) == 1:
            return tokens_ref[rows, :].astype(F32)
        given = upstream[0][rows, :] + (upstream[1][rows, :].astype(F32) + upstream[2][rows, :].astype(F32))
        given_ref[rows, :] = given
        return given

    norm_back_tiles(given_of, normal, inverse, gain, grad_ref, low_ref, sums_ref)
    keep_half(low_ref, section[0], half_ref)


def feed_back_kernel(layout, scalars, ins, hidden_ref, sums_ref, *part_refs):
    sources, slope, blocks = ins
    ups, downs = layout.named("up"), layout.named("down")
    row_count, col_count, width = len(blocks), len(blocks[0]), layout.width
    sums_ref[...] = jnp.zeros_like(sums_ref)
    begin = 0
    for source, part_ref in zip(sources, part_refs):
        count = source.shape[0]

        def through(rows, source=source, begin=begin):
            held = source[rows, :]
            here = pl.ds(begin + rows.start, rows.size)
            for j in range(col_count):
                terms = []
                for i in range(row_count):
                    for slab in downs:
                        start = (i * len(downs) + slab.number) * width
                        terms.append(dot_nt(held[:, start : start + width], take_slab(blocks[i][j], slab)))
                result = add_up(terms)
                span = slice(j * result.shape[1], (j + 1) * result.shape[1])
                grad = (result * slope[here, span].astype(F32)).astype(LOW)
                hidden_ref[here, span] = grad
                sums_ref[0:1, span] += jnp.sum(grad.astype(F32), axis=0, keepdims=True)

        each_tile(count, TILE, through)

        def back(rows, begin=begin, part_ref=part_ref):
            held = hidden_ref[pl.ds(begin + rows.start, rows.size), :]
            for i in range(row_count):
                terms = []
                for j in range(col_count):
                    for slab in ups:
                        start = (j * len(ups) + slab.number) * width
                        terms.append(dot_nt(held[:, start : start + width], take_slab(blocks[i][j], slab)))
                result = add_up(terms)
                part_ref[rows, i * result.shape[1] : (i + 1) * result.shape[1]] = result.astype(LOW)

        each_tile(count, TILE, back)
        begin += count


def attend_back_kernel(
    layout, scalars, ins, grad_ref, low_ref, packed_ref, part_ref, sums_ref, bias_sums_ref, context_ref
):
    (section,) = scalars
    above, own, came, mine, others, normal, inverse, gain, queries, keys, values, probs, blocks = ins
    slots, half = queries.shape
    row_count, col_count, width = len(blocks), len(blocks[0]), layout.width

    def given_of(rows):
        return above[rows, :] + branch_tile(rows, own, came, mine, others, section[0])

    norm_back_tiles(given_of, normal, inverse, gain, grad_ref, low_ref, sums_ref)

    def to_context(rows):
        held = low_ref[rows, :]
        slabs = layout.named("out")
        for j in range(col_count):
            terms = []
            for i in range(row_count):
                for slab in slabs:
                    start = (i * len(slabs) + slab.number) * width
                    terms.append(dot_nt(held[:, start : start + width], take_slab(blocks[i][j], slab)))
            result = add_up(terms)
            context_ref[rows, j * result.shape[1] : (j + 1) * result.shape[1]] = result.astype(LOW)

    each_tile(slots, TILE, to_context)
    factor = HD ** (-0.5)

    def heads(pair, carry):
        lanes = pl.ds(pl.multiple_of(pair * PAIR, PAIR), PAIR)
        query, key, value = queries[:, lanes], keys[:, lanes], values[:, lanes]
        grad = context_ref[:, lanes]
        grad_heads, key_heads = both_heads(grad), both_heads(key)
        grad_turned, query_turned = grad.T, query.T
        grad_queries, grad_keys, grad_values = [], [], []
        for h in range(2):
            span = slice(h * HD, (h + 1) * HD)
            tiles = []
            for start in range(0, slots, TILE):
                rows = slice(start, start + TILE)
                soft_low = probs[2 * pair + h, rows, :]
                soft = soft_low.astype(F32)
                grad_soft = dot_nt(grad_heads[h][rows], value)
                centered = jnp.sum(soft * grad_soft, axis=1, keepdims=True)
                grad_scores = (soft * (grad_soft - centered)).astype(LOW)
                tiles.append(
                    (
                        dot(grad_scores, key_heads[h]),
                        dot(query_turned[span, rows], grad_scores),
                        dot(grad_turned[span, rows], soft_low),
                    )
                )
            grad_queries.append(jnp.concatenate([tile[0] for tile in tiles], axis=0))
            grad_keys.append(add_up([tile[1] for tile in tiles]))
            grad_values.append(add_up([tile[2] for tile in tiles]))
        grad_query = (add_up(grad_queries) * factor).astype(LOW)
        grad_key = (jnp.concatenate(grad_keys, axis=0) * factor).T.astype(LOW)
        grad_value = jnp.concatenate(grad_values, axis=0).T.astype(LOW)
        for n, result in enumerate((grad_query, grad_key, grad_value)):
            packed_ref[:, pl.ds(pl.multiple_of(n * half + pair * PAIR, PAIR), PAIR)] = result
        for n, result in ((0, grad_query), (1, grad_value)):
            bias_sums_ref[n : n + 1, lanes] = jnp.sum(result.astype(F32), axis=0, keepdims=True)
        return carry

    lax.fori_loop(0, half // PAIR, heads, 0)

    def back(rows):
        held = packed_ref[rows, :]
        for i in range(row_count):
            terms = []
            for j in range(col_count):
                for n, name in enumerate(("query", "key", "value")):
                    for slab in layout.named(name):
                        start = n * half + j * (half // col_count) + slab.number * width
                        terms.append(dot_nt(held[:, start : start + width], take_slab(blocks[i][j], slab)))
            result = add_up(terms)
            part_ref[rows, i * result.shape[1] : (i + 1) * result.shape[1]] = result.astype(LOW)

    each_tile(slots, TILE, back)


def all_tokens(segments, lanes):
    if len(segments) == 1:
        return segments[0][:, lanes]
    return jnp.concatenate([segment[:, lanes] for segment in segments], axis=0)


def weight_kernel(layout, grid, plan, axis, scalars, ins, *refs):
    row_count, col_count = grid

    def store(slab, i, j, tile, value):
        value = value.astype(LOW)
        rows = pl.ds(slab.start + tile, value.shape[0])
        if axis is None:
            refs[0][i, j, rows, :] = value
        elif axis == "rows":
            lower = slab.start // (layout.height // 2)
            rows = pl.ds(slab.start % (layout.height // 2) + tile, value.shape[0])
            refs[i][lower, rows, :] = value
        else:
            height = layout.height // len(axis)
            chunk = slab.start // height
            away, other = (i, j) if axis[chunk] == "row" else (j, i)
            refs[2 * chunk + away][other, pl.ds(slab.start % height + tile, value.shape[0]), :] = value

    if len(ins) > 4:
        for ref in refs[:2]:
            for b in range(ref.shape[0]):
                ref[b, layout.height // len(axis) :, :] = ins[4][...]
    done = []
    for slab in layout.slabs:
        left, right, right_start, left_by_row = plan[slab.name]
        if (left, left_by_row) in done:
            continue
        done.append((left, left_by_row))
        sharing = [s for s in layout.slabs if plan[s.name][0] == left and plan[s.name][3] == left_by_row]
        height = slab.height
        tile = min(TILE, height)
        outer, inner = (row_count, col_count) if left_by_row else (col_count, row_count)
        for a in range(outer):

            def step(number, carry, a=a, sharing=sharing, tile=tile, height=height, left=left):
                start = pl.multiple_of(number * tile, tile)
                turned = all_tokens(ins[left], pl.ds(pl.multiple_of(a * height + start, tile), tile)).T
                for s in sharing:
                    _, right, right_start, by_row = plan[s.name]
                    count = sum(t.name == s.name for t in layout.slabs)
                    for b in range(inner):
                        column = right_start + (b * count + s.number) * layout.width
                        value = dot(turned, all_tokens(ins[right], slice(column, column + layout.width)))
                        i, j = (a, b) if by_row else (b, a)
                        store(s, i, j, start, value)
                return carry

            lax.fori_loop(0, height // tile, step, 0)


def collect_kernel(scalars, ins, stored_ref, total_ref):
    section, place = scalars
    first, own, came, second = ins

    @pl.when(section[0] == 0)
    def _():
        def step(rows):
            total_ref[rows, :] = first[rows, :] + (own[rows, :].astype(F32) + came[rows, :].astype(F32))

        each_tile(first.shape[0], NORM_TILE, step)
        pack(total_ref, place[0], stored_ref)

    @pl.when(section[0] != 0)
    def _():
        pack(second, place[0], stored_ref)


def attend_forward(inputs, lengths, place, layout, attn, small):
    half, width = small["query_bias"].shape[1], small["out_bias"].shape[1]
    tokens = inputs.shape[0] if inputs.ndim == 2 else 2 * inputs.shape[1]
    low = lambda n: shaped((tokens, n), LOW)
    results = launch(
        functools.partial(attend_kernel, layout),
        ((low(width),) if inputs.ndim == 3 else ())
        + (low(half), low(half), low(half), shaped((half // HD, tokens, tokens), LOW), low(half), low(width)),
        (inputs, small["query_bias"], small["value_bias"], attn),
        flops=8 * tokens * width * half + 16 * tokens * tokens * half,
        scalars=(lengths, place),
    )
    return results if inputs.ndim == 3 else [inputs, *results]


def norm_forward(inputs, own, came, section_at, small):
    tokens, width = inputs.shape
    low, high = (lambda n: shaped((tokens, n), LOW)), (lambda n: shaped((tokens, n), F32))
    return launch(
        norm_kernel,
        (high(width), low(width), shaped((tokens // 2, width), LOW), low(width), high(1)),
        (inputs, own, came, small["out_bias"], small["norm1_gain"], small["norm1_shift"]),
        scalars=(section_at,),
    )


def feed_forward(sources, layout, feed, small):
    width, hidden = sources[0].shape[1], small["up_bias"].shape[1]
    tokens = sum(source.shape[0] for source in sources)
    parts = tuple(shaped(source.shape, LOW) for source in sources)
    return launch(
        functools.partial(feed_kernel, layout),
        (shaped((tokens, hidden), LOW), shaped((tokens, hidden), LOW), *parts),
        (sources, small["up_bias"], feed),
        flops=4 * tokens * width * hidden,
    )


def finish_forward(normed, own, came, mine, others, section_at, place, small):
    tokens, width = normed.shape
    grid = lax.axis_size("row") * lax.axis_size("col")
    low = lambda n: shaped((tokens, n), LOW)
    return launch(
        finish_kernel,
        (low(width), shaped((grid, tokens // 4, 2 * width // grid), LOW), low(width), shaped((tokens, 1), F32)),
        (normed, own, came, mine, others, small["down_bias"], small["norm2_gain"], small["norm2_shift"]),
        scalars=(section_at, place),
    )


def weight_grads(layout, plan, operands, tokens, axis):
    row_count, col_count = lax.axis_size("row"), lax.axis_size("col")
    height, width = layout.height, layout.width
    if axis == "rows":
        col_count = 1
        outputs = (shaped((2, height // 2, width), LOW),) * row_count
    elif small_grid():
        extra = [operands[4].shape[0], *[0] * (len(axis) - 1)]
        outputs = [shaped((2, height // len(axis) + more, width), LOW) for more in extra for _ in range(2)]
    else:
        axis = None
        outputs = (shaped((row_count, col_count, height, width), LOW),)
    return launch(
        functools.partial(weight_kernel, layout, (row_count, col_count), plan, axis),
        outputs,
        operands,
        flops=2 * tokens * height * width * row_count * col_count,
    )


def norm_two_back(upstream, normal, inverse, section_at, place, small):
    tokens, width = normal.shape
    low, high = (lambda n: shaped((tokens, n), LOW)), (lambda n: shaped((tokens, n), F32))
    given = (high(width),) if len(upstream) > 1 else ()
    *given, grad, branch_low, half_low, sums = launch(
        norm_two_back_kernel,
        (*given, high(width), low(width), shaped((tokens // 2, width), LOW), shaped((8, width), F32)),
        (upstream, normal, inverse, small["norm2_gain"]),
        scratch=() if given else (pltpu.VMEM((tokens, width), LOW),),
        scalars=(section_at, place),
    )
    return given, grad, branch_low, half_low, sums


def feed_back(sources, slope, layout, feed):
    tokens, hidden = slope.shape
    width = sources[0].shape[1]
    parts = tuple(shaped(source.shape, LOW) for source in sources)
    return launch(
        functools.partial(feed_back_kernel, layout),
        (shaped((tokens, hidden), LOW), shaped((8, hidden), F32), *parts),
        (sources, slope, feed),
        flops=4 * tokens * width * hidden,
    )


def attend_back(above, parts, normal, inverse, queries, keys, values, probs, section_at, layout, attn, small):
    tokens, width = normal.shape
    half = queries.shape[1]
    low, high = (lambda n: shaped((tokens, n), LOW)), (lambda n: shaped((tokens, n), F32))
    grad, attended_low, packed, own, sums, bias_sums = launch(
        functools.partial(attend_back_kernel, layout),
        (high(width), low(width), low(3 * half), low(width), shaped((8, width), F32), shaped((8, half), F32)),
        (above, *parts, normal, inverse, small["norm1_gain"], queries, keys, values, probs, attn),
        scratch=[pltpu.VMEM((tokens, half), LOW)],
        flops=8 * tokens * width * half + 32 * tokens * tokens * half,
        scalars=(section_at,),
    )
    grads = {"norm1_gain": sums[0], "norm1_shift": sums[1], "out_bias": sums[2]}
    grads |= {"query_bias": bias_sums[0], "value_bias": bias_sums[1]}
    return grad, attended_low, packed, own, grads


FEED_PLAN = {"up": (0, 1, 0, True), "down": (2, 3, 0, False)}


def attn_plan(half):
    return {
        "query": (0, 1, 0, True),
        "key": (0, 1, half, True),
        "value": (0, 1, 2 * half, True),
        "out": (2, 3, 0, False),
    }


HALVED = ("query_bias", "value_bias", "up_bias")
WHOLE = ("out_bias", "norm1_gain", "norm1_shift", "down_bias", "norm2_gain", "norm2_shift")


def body(
    tokens_in,
    lengths,
    placement,
    cotangent,
    qkv_weight,
    qv_bias,
    out_weight,
    out_bias,
    norm1_gain,
    norm1_shift,
    up_weight,
    up_bias,
    down_weight,
    down_bias,
    norm2_gain,
    norm2_shift,
):
    row_count, col_count = lax.axis_size("row"), lax.axis_size("col")
    grid = row_count * col_count
    section, group = lax.axis_index("section"), lax.axis_index("dp")
    row, col = lax.axis_index("row"), lax.axis_index("col")
    is_first = section == 0
    seq_local, half_slots, _, packed_width = tokens_in.shape
    if seq_local != grid or col_count != 2 or lax.axis_size("dp") != 4:
        raise ValueError("unexpected grid")
    features = packed_width // 2
    seq_total = placement.shape[0]
    width = features * grid
    section_at, place = section.reshape(1), row.reshape(1)

    attn_layout = make_layout(
        [(name, qkv_weight.shape[2], qkv_weight.shape[3] // 2) for name in ("query", "key", "value")]
        + [("out", out_weight.shape[1] // 2, out_weight.shape[2])]
    )
    feed_layout = make_layout(
        [("up", up_weight.shape[1], up_weight.shape[2] // 2), ("down", down_weight.shape[1] // 2, down_weight.shape[2])]
    )

    def exchange(stored):
        return lax.all_to_all(stored, ("row", "col"), split_axis=0, concat_axis=0, tiled=True)

    def both_layers(layout, operands, sources):
        piece = shaped((layout.height, layout.width), LOW)
        stays, leaves = launch(
            functools.partial(halves_kernel, layout, sources), (piece, piece), operands, scalars=(section_at,)
        )
        came = swap_section(leaves)
        return jnp.where(is_first, stays, came), jnp.where(is_first, came, stays)

    attn_pieces = both_layers(
        attn_layout,
        (qkv_weight[0], out_weight[0]),
        {
            "query": (lambda ins: ins[0].at[0], False),
            "key": (lambda ins: ins[0].at[1], False),
            "value": (lambda ins: ins[0].at[2], False),
            "out": (lambda ins: ins[1], True),
        },
    )
    attn_near = gather_first(attn_pieces[0])
    inputs = exchange(tokens_in[:, :, 0])
    attn_near = after(attn_near, inputs)
    feed_pieces = both_layers(
        feed_layout,
        (after(up_weight[0], attn_pieces), down_weight[0]),
        {"up": (lambda ins: ins[0], False), "down": (lambda ins: ins[1], True)},
    )
    small_own = (qv_bias, up_bias, out_bias, norm1_gain, norm1_shift, down_bias, norm2_gain, norm2_shift)
    sizes = [t.size for t in small_own]
    flat = jnp.concatenate([t.reshape(-1) for t in small_own])
    padded = -(-flat.size // 2048) * 2048
    flat = jnp.pad(flat, (0, padded - flat.size)).reshape(-1, 128)
    flat_near = gather_first(flat)
    flat_blocks = gather_second(flat, flat_near, "row")
    flat_own = jnp.stack([jnp.stack([jnp.concatenate(b).reshape(-1) for b in line]) for line in flat_blocks])
    flat_own = jnp.roll(flat_own, col, axis=1)
    flat_other = swap_section(flat_own.reshape(-1, 128)).reshape(flat_own.shape)
    flat_all = [jnp.where(is_first, flat_own, flat_other), jnp.where(is_first, flat_other, flat_own)]
    starts = [sum(sizes[:n]) for n in range(len(sizes) + 1)]

    def own_part(by_col, count, which):
        halves = by_col.reshape(*by_col.shape[:-1], count, -1)
        chosen = lax.dynamic_index_in_dim(halves, which, axis=halves.ndim - 2, keepdims=False)
        return jnp.roll(chosen, -col, axis=-2) if chosen.shape[-2] > 1 else chosen

    smalls = []
    for layer in range(2):
        fields = [flat_all[layer][..., starts[n] : starts[n + 1]] for n in range(len(sizes))]
        rows_first = [jnp.roll(field, row, axis=0) for field in fields[:2]]
        qv = rows_first[0].reshape(row_count, col_count, 2, -1).transpose(2, 1, 0, 3)
        qv = own_part(qv.reshape(2, col_count, -1), 2, section).reshape(2, -1)
        up_shift = rows_first[1].transpose(1, 0, 2).reshape(col_count, -1)
        up_shift = lax.dynamic_index_in_dim(up_shift, col, axis=0)
        up_shift = own_part(up_shift, 2, section).reshape(1, -1)
        small = {"query_bias": qv[:1], "value_bias": qv[1:], "up_bias": up_shift}
        for name, field in zip(WHOLE, fields[2:]):
            small[name] = field.reshape(1, -1)
        smalls.append(small)

    own_lengths = lax.dynamic_slice_in_dim(lengths, group * seq_local + row * col_count + col, 1)

    cot_all = lax.all_gather(cotangent[:, :, 0], "dp", axis=0, tiled=True)
    wanted = group * seq_local + lax.broadcasted_iota(jnp.int32, (seq_local,), 0)
    matches = placement[None, :] == wanted[:, None]
    position = jnp.sum(
        jnp.where(matches, lax.broadcasted_iota(jnp.int32, (seq_local, seq_total), 1), 0), axis=1
    )
    cot_held = jnp.take(cot_all, position, axis=0)

    attn_first = gather_second(attn_pieces[0], attn_near, "col")
    feed_first = gather_rows(after(feed_pieces[0], attn_near, flat_blocks))
    small = smalls[0]
    def to_dealt(stored):
        held = lax.all_gather(exchange(stored), "dp", axis=0, tiled=True)
        return jnp.take(held, lax.dynamic_slice_in_dim(placement, group * seq_local, seq_local), axis=0)

    near = after(attn_pieces[1], attn_first)
    near = fetch(near, "col", 1) if small_grid() else gather_first(near)
    inputs, *attended_first, own = attend_forward(inputs, own_lengths, place, attn_layout, attn_first, small)
    came = swap_section(own)
    normed, low, half_low, *normed_first = norm_forward(inputs, own, came, section_at, small)
    got = pair_col(half_low)
    feed_first = after(feed_first, half_low)
    active, slope, own = feed_forward([low], feed_layout, feed_first, small)
    came = swap_section(own)
    pair_low = both_halves(got, own, near)
    far = fetch(after(attn_pieces[1], feed_first), "row", 1) if small_grid() else near
    pair_active, pair_slope, mine, others = feed_forward(pair_low, feed_layout, feed_first, small)
    fed_first = ([low, *pair_low], [active, pair_active], (slope, pair_slope))
    mine, others = both_halves(to_pair(mine, others), far)
    attn_second = gather_second(attn_pieces[1], after((far, near), own) if small_grid() else near, "row")
    feed_second = gather_rows(after(feed_pieces[1], attn_second))
    middle, first_stored, *finished_first = finish_forward(normed, own, came, mine, others, section_at, place, small)
    small = smalls[1]
    first_dealt = to_dealt(first_stored)
    _, *attended_second, own = attend_forward(middle, own_lengths, place, attn_layout, attn_second, small)
    came = swap_section(own)
    normed, low, half_low, *normed_second = norm_forward(middle, own, came, section_at, small)
    got = pair_col(half_low)
    feed_second = after(feed_second, half_low)
    active, slope, own = feed_forward([low], feed_layout, feed_second, small)
    came = swap_section(own)
    pair_low = both_halves(got, own)
    upstream = exchange(after(cot_held, pair_low))
    pair_active, pair_slope, mine, others = feed_forward(pair_low, feed_layout, feed_second, small)
    fed_second = ([low, *pair_low], [active, pair_active], (slope, pair_slope))
    mine, others = both_halves(to_pair(mine, others))
    _, second_stored, *finished_second = finish_forward(normed, own, came, mine, others, section_at, place, small)

    def small_rows(grads):
        up = grads["up_bias"].reshape(1, -1)
        up = jnp.concatenate([up, *[jnp.zeros_like(up)] * (col_count - 1)])
        grads = grads | {"up_bias": up}
        parts = [jnp.roll(grads[name].reshape(col_count, -1), col, axis=0).reshape(-1) for name in HALVED]
        parts += [jnp.roll(grads[name].reshape(row_count, -1), row, axis=0).reshape(-1) for name in WHOLE]
        vector = jnp.concatenate(parts)
        lanes = attn_layout.width
        count = -(-vector.size // (16 * lanes)) * 16
        return jnp.pad(vector, (0, count * lanes - vector.size)).reshape(count, lanes)

    axes = ("row", "col")

    def attn_grads(source, attended, attended_low, packed, small):
        operands = ([source], [packed], [attended[4]], [attended_low])
        small = small_rows(small)
        if small_grid():
            operands = (*operands, small.astype(LOW))
        parts = weight_grads(attn_layout, attn_plan(width // 2), operands, 2 * half_slots, axes)
        return ([parts[:2], parts[2:]] if small_grid() else [parts]), small

    def all_first(parts):
        return [scatter_first(part, axis) for part, axis in zip(parts, axes)]

    def all_middle(parts, moved):
        return [scatter_middle(*both) for both in zip(parts, moved)]

    def all_second(middles):
        return [scatter_second(middle, axis) for middle, axis in zip(middles, axes)]

    def all_last(parts, middles, seconds, small):
        totals = [scatter_last(*each) for each in zip(parts, middles, seconds)]
        if small_grid():
            return totals
        return [jnp.concatenate([*totals, lax.psum(small, ("row", "col")).astype(LOW)])]

    def all_add(totals, came):
        return [add_low(*both) for both in zip(totals, came)]

    def feed_weights(fed, branches, hiddens):
        lows, actives, _ = fed
        return weight_grads(feed_layout, FEED_PLAN, (lows, hiddens, actives, branches), 4 * half_slots, "rows")

    small = smalls[1]
    _, grad, branch_low, half_low, sums = norm_two_back(
        (upstream,), *finished_second, section_at, place, small
    )
    got = pair_col(half_low)
    hidden, hidden_sums, own = feed_back([branch_low], fed_second[2][0], feed_layout, feed_second)
    came = swap_section(own)
    pair_low = both_halves(got, own)
    second_dealt = to_dealt(after(second_stored, pair_low, first_dealt))
    pair_hidden, pair_sums, mine, others = feed_back(pair_low, fed_second[2][1], feed_layout, feed_second)
    got = to_pair(mine, others)
    small_grads = {"norm2_gain": sums[0], "norm2_shift": sums[1], "down_bias": sums[2]}
    small_grads["up_bias"] = hidden_sums[0] + pair_sums[0]
    parts_second = feed_weights(fed_second, [branch_low, *pair_low], [hidden, pair_hidden])
    mine, others = both_halves(got, parts_second)
    came_second = rows_sent(parts_second)
    grad, attended_low, packed, own, more = attend_back(
        grad, (own, came, mine, others), *normed_second, *attended_second[:4], section_at, attn_layout, attn_second, small
    )
    came = swap_section(own)
    small_second = small_grads | more
    small = smalls[0]
    given, grad, branch_low, half_low, sums = norm_two_back(
        (grad, own, came), *finished_first, section_at, place, small
    )
    got = pair_col(half_low)
    attn_parts_second, rows_second = attn_grads(
        middle, attended_second, after(attended_low, half_low), packed, small_second
    )
    came_second = after(came_second, attn_parts_second)
    up_second, down_second = (rows_sum(parts_second, came_second, half) for half in range(2))
    up_in, down_in = group_in(up_second), group_in(down_second)
    attn_moved_second = all_first(after(attn_parts_second, down_second))
    branch_low = after(branch_low, up_second, down_second)
    hidden, hidden_sums, own = feed_back([branch_low], fed_first[2][0], feed_layout, feed_first)
    came = swap_section(own)
    pair_low = both_halves(got, own)
    pair_hidden, pair_sums, mine, others = feed_back(pair_low, fed_first[2][1], feed_layout, feed_first)
    got = to_pair(mine, others)
    up_second = add_low(up_second, after(up_in, pair_hidden))
    up_across = group_across(up_second)
    attn_middle_second = all_middle(attn_parts_second, after(attn_moved_second, pair_hidden))
    attn_far_second = all_second(attn_middle_second)
    small_grads = {"norm2_gain": sums[0], "norm2_shift": sums[1], "down_bias": sums[2]}
    small_grads["up_bias"] = hidden_sums[0] + pair_sums[0]
    parts_first = feed_weights(fed_first, [branch_low, *pair_low], [hidden, after(pair_hidden, up_second, attn_middle_second)])
    came_first = rows_sent(parts_first)
    down_second = add_low(down_second, after(down_in, parts_first))
    down_across = group_across(down_second)
    mine, others = both_halves(got, parts_first)
    attn_second = all_last(attn_parts_second, attn_middle_second, after(attn_far_second, parts_first), rows_second)
    attn_in = [group_in(part) for part in attn_second]
    mine = after(mine, down_second, attn_second, second_dealt)
    grad, attended_low, packed, own, more = attend_back(
        grad, (own, came, mine, others), *normed_first, *attended_first[:4], section_at, attn_layout, attn_first, small
    )
    came = swap_section(own)
    small_first = small_grads | more

    in_middle = (group == 1) | (group == 2)

    def settled(total, outward):
        return jnp.where(in_middle, total, outward)

    def all_settled(totals, outwards):
        return [settled(*both) for both in zip(totals, outwards)]

    attn_second = all_add(attn_second, after(attn_in, own))
    attn_across = [group_across(part) for part in attn_second]
    up_second = add_low(up_second, after(up_across, attn_second))
    up_out_second = group_out(up_second)
    attn_parts_first, rows_first = attn_grads(
        inputs, attended_first, after(attended_low, up_second), packed, small_first
    )
    attn_moved_first = all_first(attn_parts_first)
    (stored_grad,) = launch(
        collect_kernel,
        (shaped((grid, half_slots, packed_width), F32),),
        (after(grad, attn_parts_first), own, came, *given),
        scratch=[pltpu.VMEM((2 * half_slots, width), F32)],
        scalars=(section_at, place),
    )
    came_first = after(came_first, stored_grad)
    up_first, down_first = (rows_sum(parts_first, came_first, half) for half in range(2))
    up_in, down_in = group_in(up_first), group_in(down_first)
    down_second = add_low(down_second, after(down_across, up_first, down_first))
    down_out_second = group_out(down_second)
    up_second = settled(up_second, after(up_out_second, down_second))
    attn_second = all_add(attn_second, after(attn_across, up_second))
    attn_out_second = [group_out(part) for part in attn_second]
    attn_middle_first = all_middle(attn_parts_first, after(attn_moved_first, attn_second))
    attn_far_first = all_second(attn_middle_first)
    up_first = add_low(up_first, after(up_in, attn_middle_first))
    up_across = group_across(up_first)
    down_second = settled(down_second, after(down_out_second, up_first))
    attn_first = all_last(attn_parts_first, attn_middle_first, after(attn_far_first, down_second), rows_first)
    last_in = [group_in(part) for part in attn_first]
    down_first = add_low(down_first, after(down_in, attn_first))
    down_across = group_across(down_first)
    up_first = add_low(up_first, after(up_across, down_first))
    up_out_first = group_out(up_first)
    attn_second = all_settled(attn_second, after(attn_out_second, up_first))
    input_grad = exchange(after(stored_grad, attn_second))
    attn_first = all_add(attn_first, after(last_in, attn_second))
    last_across = [group_across(part) for part in attn_first]

    first_dealt, second_dealt = after((first_dealt, second_dealt), attn_first)
    own_half = jnp.where(is_first, first_dealt, second_dealt)
    other_half = swap_section(jnp.where(is_first, second_dealt, first_dealt))
    layer_out = jnp.concatenate(
        [jnp.where(is_first, own_half, other_half), jnp.where(is_first, other_half, own_half)], axis=1
    )
    down_first = add_low(down_first, after(down_across, attn_first))
    down_out_first = group_out(down_first)
    up_first = settled(up_first, after(up_out_first, down_first, layer_out, input_grad))
    attn_first = all_add(attn_first, after(last_across, up_first))
    last_out = [group_out(part) for part in attn_first]
    down_first = settled(down_first, after(down_out_first, attn_first))

    feed_second, feed_first = [up_second, down_second], [up_first, down_first]

    def to_section(first, second):
        return jnp.where(is_first, first, second), swap_section(jnp.where(is_first, second, first))

    feed_stays, feed_came = zip(*[to_section(a, b) for a, b in zip(feed_first, feed_second)])
    up_grad, down_grad = launch(
        functools.partial(
            whole_kernel, feed_layout, {"up": (lambda refs: refs[0], False), "down": (lambda refs: refs[1], True)}
        ),
        (shaped(up_weight.shape[1:], F32), shaped(down_weight.shape[1:], F32)),
        (feed_stays, feed_came),
        scalars=(section_at,),
    )
    attn_first = all_settled(attn_first, after(last_out, up_grad, down_grad))
    attn_stays, attn_came = zip(*[to_section(a, b) for a, b in zip(attn_first, attn_second)])

    qkv_grad, out_grad = launch(
        functools.partial(
            whole_kernel,
            attn_layout,
            {
                "query": (lambda refs: refs[0].at[0], False),
                "key": (lambda refs: refs[0].at[1], False),
                "value": (lambda refs: refs[0].at[2], False),
                "out": (lambda refs: refs[1], True),
            },
        ),
        (shaped(qkv_weight.shape[1:], F32), shaped(out_weight.shape[1:], F32)),
        (attn_stays, attn_came),
        scalars=(section_at,),
    )

    lasting = 2 * (width // 2) + up_bias.size * grid // 2 + len(WHOLE) * width
    held = attn_layout.height // len(attn_first)
    small_stays, small_came = (t[0][held:].reshape(-1)[:lasting].astype(F32) for t in (attn_stays, attn_came))
    small_halves = jnp.stack(
        [jnp.where(is_first, small_stays, small_came), jnp.where(is_first, small_came, small_stays)]
    )
    model, hidden = width // 2, up_bias.size * grid // 2
    ends = (0, model, 2 * model, 2 * model + hidden)

    def own_col_row(begin, end):
        blocks = small_halves[:, begin:end].reshape(2, col_count, -1).transpose(1, 0, 2)
        blocks = blocks.reshape(col_count * row_count, -1)
        return lax.dynamic_index_in_dim(blocks, col * row_count + row, axis=0, keepdims=False)

    query_sum, value_sum, up_sum = (own_col_row(ends[n], ends[n + 1]) for n in range(3))
    qv_grad = jnp.stack([query_sum, value_sum]).reshape(qv_bias.shape)
    up_bias_grad = up_sum.reshape(up_bias.shape)
    rest = small_halves[0, ends[3] :].reshape(len(WHOLE), grid, features)
    rest = lax.dynamic_index_in_dim(rest, row * col_count + col, axis=1, keepdims=False)
    whole_grads = {name: rest[n][None] for n, name in enumerate(WHOLE)}
    return (
        layer_out[None, :, :, None],
        input_grad[None, :, :, None],
        qkv_grad[None],
        qv_grad,
        out_grad[None],
        whole_grads["out_bias"],
        whole_grads["norm1_gain"],
        whole_grads["norm1_shift"],
        up_grad[None],
        up_bias_grad,
        down_grad[None],
        whole_grads["down_bias"],
        whole_grads["norm2_gain"],
        whole_grads["norm2_shift"],
    )


def solution(mesh):
    tokens = P("dp", None, ("row", "col"), None)
    feature = P("section", ("row", "col"))
    outward = P("section", "col", "row")
    hidden = P("section", "col", "row", None)
    qv = P("section", None, "col", "row", None)
    stored = P("section", "dp", None, ("row", "col"), None)
    inward = P("section", "row", "col")
    qkv = P("section", None, "row", "col")
    params = (
        qkv, qv, outward, feature, feature, feature, inward, hidden, outward, feature, feature, feature,
    )
    return jax.shard_map(
        body,
        mesh=mesh,
        in_specs=(tokens, P(), P(), tokens, *params),
        out_specs=(stored, stored, *params),
        check_vma=False,
    )
```

```python
import functools
from typing import NamedTuple

import jax
import jax.numpy as jnp
from jax import lax
from jax.experimental import pallas as pl
from jax.experimental.pallas import tpu as pltpu
from jax.sharding import PartitionSpec as P

HD = 64
PAIR = 2 * HD
EPSILON = 1e-05
MASKED = -1000000000.0
F32 = jnp.float32
LOW = jnp.bfloat16
COST = 0.02
VMEM_LIMIT = 56 * 1024 * 1024
TILE = 512
NORM_TILE = 512


def dot(left, right):
    return lax.dot_general(left, right, (((1,), (0,)), ((), ())), preferred_element_type=F32)


def dot_nt(left, right):
    return lax.dot_general(left, right, (((1,), (1,)), ((), ())), preferred_element_type=F32)


def shaped(shape, dtype):
    return jax.ShapeDtypeStruct(shape, dtype)


def fetch(value, axis, steps):
    count = lax.axis_size(axis)
    return lax.ppermute(value, axis, [((place + steps) % count, place) for place in range(count)])


def send(value, axis, steps):
    count = lax.axis_size(axis)
    return lax.ppermute(value, axis, [(place, (place + steps) % count) for place in range(count)])


def swap_section(value):
    return lax.ppermute(value, "section", [(0, 1), (1, 0)])


def after(value, *others):
    return lax.optimization_barrier((value, others))[0]


def small_grid():
    return lax.axis_size("row") == 2 and lax.axis_size("col") == 2


def gather_rows(piece):
    return [[[piece]]] + [[[fetch(piece, "row", i)]] for i in range(1, lax.axis_size("row"))]


def gather_first(piece):
    if small_grid():
        return fetch(piece, "row", 1), fetch(piece, "col", 1)
    blocks = []
    for i in range(lax.axis_size("row")):
        own = piece if i == 0 else fetch(piece, "row", i)
        blocks.append([[own if j == 0 else fetch(own, "col", j)] for j in range(lax.axis_size("col"))])
    return blocks


def gather_second(piece, first, axis):
    if not small_grid():
        return first
    far, near = first
    corner = fetch(far, "col", 1) if axis == "col" else fetch(near, "row", 1)
    return [[[piece], [near]], [[far], [corner]]]


def gather_blocks(piece):
    return gather_second(piece, gather_first(piece), "col")


def add_low(left, right):
    return (left.astype(F32) + right.astype(F32)).astype(LOW)


def rows_sent(parts):
    return [send(parts[i], "row", i) for i in range(1, len(parts))]


def rows_sum(parts, came):
    return add_up([part.astype(F32) for part in (parts[0], *came)]).astype(LOW)


def scatter_first(parts, axis):
    return send(parts[1], axis, 1) if small_grid() else ()


def scatter_middle(parts, first):
    return [add_low(parts[0][n], first[n]) for n in range(2)] if small_grid() else ()


def scatter_second(middle, axis):
    return send(middle[1], "row" if axis == "col" else "col", 1) if small_grid() else ()


def scatter_last(parts, middle, second):
    if small_grid():
        return add_low(middle[0], second)
    (blocks,) = parts
    total = blocks[0, 0].astype(F32)
    for i in range(lax.axis_size("row")):
        for j in range(lax.axis_size("col")):
            if i or j:
                block = blocks[i, j]
                block = send(block, "row", i) if i else block
                block = send(block, "col", j) if j else block
                total = total + block.astype(F32)
    return total.astype(LOW)


def group_in(value):
    return lax.ppermute(value, "dp", [(0, 1), (3, 2)])


def group_across(value):
    return lax.ppermute(value, "dp", [(1, 2), (2, 1)])


def group_out(value):
    return lax.ppermute(value, "dp", [(1, 0), (2, 3)])


def pair_col(value):
    return lax.ppermute(value, "col", [(0, 1), (1, 0)])


def both_halves(got, *beside):
    got = after(got, *beside)
    return got, swap_section(got)


def to_pair(mine, others):
    return pair_col(add_low(mine, swap_section(others)))


class Slab(NamedTuple):
    name: str
    number: int
    start: int
    height: int


class Layout(NamedTuple):
    width: int
    slabs: tuple

    @property
    def height(self):
        return self.slabs[-1].start + self.slabs[-1].height

    def named(self, name):
        return [slab for slab in self.slabs if slab.name == name]


def make_layout(weights):
    width = min(columns for _, _, columns in weights)
    slabs, start = [], 0
    for name, rows, columns in weights:
        for number in range(columns // width):
            slabs.append(Slab(name, number, start, rows))
            start += rows
    return Layout(width, tuple(slabs))


def take_slab(pieces, slab):
    each = min(piece.shape[0] for piece in pieces)
    start = slab.start % each
    return pieces[slab.start // each][start : start + slab.height, :]


def add_up(terms):
    return functools.reduce(jnp.add, terms)


def times_rows(left, blocks, j, slab):
    height = slab.height
    return add_up(
        [dot(left[:, i * height : (i + 1) * height], take_slab(blocks[i][j], slab)) for i in range(len(blocks))]
    )


def times_columns(left, blocks, i, slab):
    height = slab.height
    return add_up(
        [dot(left[:, j * height : (j + 1) * height], take_slab(blocks[i][j], slab)) for j in range(len(blocks[i]))]
    )


def launch(kernel, outputs, operands, scratch=(), flops=0, scalars=()):
    leaves, tree = jax.tree.flatten(operands)
    count_in, count_scalar = len(leaves), len(scalars)

    def inner(*refs):
        ins = jax.tree.unflatten(tree, refs[count_scalar : count_scalar + count_in])
        kernel(refs[:count_scalar], ins, *refs[count_scalar + count_in :])

    moved = sum(t.size * t.dtype.itemsize for t in (*leaves, *outputs))
    return pl.pallas_call(
        inner,
        out_shape=tuple(outputs),
        in_specs=[pl.BlockSpec(memory_space=pltpu.SMEM)] * count_scalar
        + [pl.BlockSpec(memory_space=pltpu.VMEM)] * count_in,
        out_specs=tuple(pl.BlockSpec(memory_space=pltpu.VMEM) for _ in outputs),
        scratch_shapes=list(scratch),
        compiler_params=pltpu.CompilerParams(vmem_limit_bytes=VMEM_LIMIT),
        cost_estimate=pl.CostEstimate(flops=int(COST * flops), bytes_accessed=int(COST * moved), transcendentals=0),
    )(*scalars, *leaves)


def each_tile(count, size, step):
    size = min(size, count)

    def visit(number, carry):
        step(pl.ds(pl.multiple_of(number * size, size), size))
        return carry

    lax.fori_loop(0, count // size, visit, 0)


def stored_places(blocks, row):
    count, _, packed = blocks.shape
    features = packed // 2
    row_count = lax.axis_size("row")
    col_count = count // row_count
    for i in range(row_count):
        turned = lax.rem(row + i, row_count)
        for j in range(col_count):
            place = (i * col_count + j) * features
            yield turned * col_count + j, slice(place, place + features)


def unpack(blocks, row, target):
    half, packed = blocks.shape[1:]
    for block, lanes in stored_places(blocks, row):
        target[:half, lanes] = blocks[block, :, : packed // 2]
        target[half:, lanes] = blocks[block, :, packed // 2 :]


def pack(source, row, blocks):
    half, packed = blocks.shape[1:]
    for block, lanes in stored_places(blocks, row):
        blocks[block, :, : packed // 2] = source[:half, lanes]
        blocks[block, :, packed // 2 :] = source[half:, lanes]


def normalize(values):
    center = jnp.mean(values, axis=1, keepdims=True)
    spread = values - center
    inverse = lax.rsqrt(jnp.mean(spread * spread, axis=1, keepdims=True) + EPSILON)
    return spread * inverse, inverse


def head_mask(shape, head):
    lane = lax.broadcasted_iota(jnp.int32, shape, 1)
    return (lane >= head * HD) & (lane < (head + 1) * HD)


def both_heads(values):
    return [jnp.where(head_mask(values.shape, h), values, jnp.zeros_like(values)) for h in range(2)]


def halves_kernel(layout, sources, scalars, ins, keep_ref, send_ref):
    section = scalars[0][0]
    for place, target in ((section, keep_ref), (1 - section, send_ref)):
        for slab in layout.slabs:
            rows = slice(slab.start, slab.start + slab.height)
            source, by_rows = sources[slab.name]
            lanes = slice(slab.number * layout.width, (slab.number + 1) * layout.width)
            if by_rows:
                start = pl.multiple_of(place * slab.height, slab.height)
                target[rows, :] = source(ins)[pl.ds(start, slab.height), lanes]
            else:
                total = len(layout.named(slab.name)) * layout.width
                start = pl.multiple_of(place * total + slab.number * layout.width, layout.width)
                target[rows, :] = source(ins)[:, pl.ds(start, layout.width)]


def whole_kernel(layout, targets, scalars, ins, *refs):
    section = scalars[0][0]
    for place, source in ((section, ins[0]), (1 - section, ins[1])):
        for slab in layout.slabs:
            value = take_slab(source, slab).astype(F32)
            target, by_rows = targets[slab.name]
            lanes = slice(slab.number * layout.width, (slab.number + 1) * layout.width)
            if by_rows:
                start = pl.multiple_of(place * slab.height, slab.height)
                target(refs)[pl.ds(start, slab.height), lanes] = value
            else:
                total = len(layout.named(slab.name)) * layout.width
                start = pl.multiple_of(place * total + slab.number * layout.width, layout.width)
                target(refs)[:, pl.ds(start, layout.width)] = value


def attend_kernel(layout, scalars, ins, *refs):
    lengths, place = scalars
    source, query_bias, value_bias, blocks = ins
    if source.ndim == 3:
        tokens_ref, *refs = refs
        unpack(source, place[0], tokens_ref)
        source = tokens_ref
    query_ref, key_ref, value_ref, probs_ref, context_ref, part_ref = refs
    slots = source.shape[0]
    columns = len(blocks[0])
    half = query_ref.shape[1]
    biases = {"query": query_bias, "key": None, "value": value_bias}
    targets = {"query": query_ref, "key": key_ref, "value": value_ref}

    def project(rows):
        held = source[rows, :]
        for j in range(columns):
            for name, target in targets.items():
                for slab in layout.named(name):
                    start = j * (half // columns) + slab.number * layout.width
                    span = slice(start, start + layout.width)
                    result = times_rows(held, blocks, j, slab)
                    if biases[name] is not None:
                        result = result + biases[name][:, span]
                    target[rows, span] = result.astype(LOW)

    each_tile(slots, TILE, project)
    length = lengths[0]

    def heads(pair, carry):
        lanes = pl.ds(pl.multiple_of(pair * PAIR, PAIR), PAIR)
        keys = key_ref[:, lanes]
        values = both_heads(value_ref[:, lanes])
        for start in range(0, slots, TILE):
            rows = slice(start, start + TILE)
            terms = []
            for h, queries in enumerate(both_heads(query_ref[rows, lanes])):
                scores = dot_nt(queries, keys) * HD ** (-0.5)
                token = lax.broadcasted_iota(jnp.int32, (1, slots), 1)
                slot = jnp.where(token < slots // 2, 2 * token, 2 * token - (slots - 1))
                scores = jnp.where(slot < length, scores, MASKED)
                exponent = jnp.exp(scores - jnp.max(scores, axis=1, keepdims=True))
                probs = (exponent / jnp.sum(exponent, axis=1, keepdims=True)).astype(LOW)
                probs_ref[2 * pair + h, rows, :] = probs
                terms.append(dot(probs, values[h]))
            context_ref[rows, lanes] = add_up(terms).astype(LOW)
        return carry

    lax.fori_loop(0, half // PAIR, heads, 0, unroll=True)

    def project_out(rows):
        held = context_ref[rows, :]
        slabs = layout.named("out")
        for i in range(len(blocks)):
            for slab in slabs:
                start = (i * len(slabs) + slab.number) * layout.width
                part_ref[rows, start : start + layout.width] = times_columns(held, blocks, i, slab).astype(LOW)

    each_tile(slots, TILE, project_out)


def keep_half(source, section, target):
    height = target.shape[0]
    target[...] = source[pl.ds(pl.multiple_of(section * height, height), height), :]


def norm_kernel(scalars, ins, normed_ref, low_ref, half_ref, normal_ref, inverse_ref):
    source, own, came, out_bias, gain, shift = ins
    tokens = source.shape[0]

    def norm(rows):
        attended = own[rows, :].astype(F32) + came[rows, :].astype(F32)
        normal, inverse = normalize(source[rows, :].astype(F32) + (attended + out_bias[...]))
        normed = normal * gain[...] + shift[...]
        normed_ref[rows, :] = normed
        low_ref[rows, :] = normed.astype(LOW)
        normal_ref[rows, :] = normal.astype(LOW)
        inverse_ref[rows, :] = inverse

    each_tile(tokens, NORM_TILE, norm)
    keep_half(low_ref, scalars[0][0], half_ref)


def feed_kernel(layout, scalars, ins, active_ref, slope_ref, *part_refs):
    sources, up_bias, blocks = ins
    ups, downs = layout.named("up"), layout.named("down")
    first = 0
    for source, part_ref in zip(sources, part_refs):
        count = source.shape[0]

        def widen(rows, source=source, first=first):
            held = source[rows, :]
            here = pl.ds(first + rows.start, rows.size)
            for j in range(len(blocks[0])):
                for slab in ups:
                    start = (j * len(ups) + slab.number) * layout.width
                    span = slice(start, start + layout.width)
                    preact = times_rows(held, blocks, j, slab) + up_bias[:, span]
                    cdf = 0.5 * (1.0 + lax.erf(preact * 2.0 ** (-0.5)))
                    density = jnp.exp(-0.5 * preact * preact) * (2.0 * jnp.pi) ** (-0.5)
                    active_ref[here, span] = (preact * cdf).astype(LOW)
                    slope_ref[here, span] = (cdf + preact * density).astype(LOW)

        each_tile(count, TILE, widen)

        def narrow(rows, first=first, part_ref=part_ref):
            held = active_ref[pl.ds(first + rows.start, rows.size), :]
            for i in range(len(blocks)):
                for slab in downs:
                    start = (i * len(downs) + slab.number) * layout.width
                    part_ref[rows, start : start + layout.width] = times_columns(held, blocks, i, slab).astype(LOW)

        each_tile(count, TILE, narrow)
        first += count


def branch_tile(rows, own, came, mine, others, section):
    total = own[rows, :].astype(F32) + came[rows, :].astype(F32)
    height = mine.shape[0]
    inner = pl.ds(lax.rem(rows.start, height), rows.size)
    in_mine = rows.start // height == section
    pair = jnp.where(in_mine, mine[inner, :].astype(F32), others[inner, :].astype(F32))
    return total + pair


def finish_kernel(scalars, ins, output_ref, stored_ref, normal_ref, inverse_ref):
    section, place = scalars
    normed, own, came, mine, others, bias, gain, shift = ins

    def norm(rows):
        branch = branch_tile(rows, own, came, mine, others, section[0])
        normal, inverse = normalize(normed[rows, :] + (branch + bias[...]))
        output_ref[rows, :] = (normal * gain[...] + shift[...]).astype(LOW)
        normal_ref[rows, :] = normal.astype(LOW)
        inverse_ref[rows, :] = inverse

    each_tile(normed.shape[0], min(NORM_TILE, mine.shape[0]), norm)
    half, packed = stored_ref.shape[1:]
    first = pl.ds(pl.multiple_of(section[0] * half, half), half)
    second = pl.ds(pl.multiple_of(2 * half + section[0] * half, half), half)
    for block, lanes in stored_places(stored_ref, place[0]):
        stored_ref[block, :, : packed // 2] = output_ref[first, lanes]
        stored_ref[block, :, packed // 2 :] = output_ref[second, lanes]


def norm_back(upstream, normal, inverse, gain):
    scaled = upstream * gain
    first = jnp.mean(scaled, axis=1, keepdims=True)
    second = jnp.mean(scaled * normal, axis=1, keepdims=True)
    return inverse * (scaled - first - normal * second)


def norm_back_tiles(given_of, normal, inverse, gain, grad_ref, low_ref, sums_ref, size=NORM_TILE):
    sums_ref[...] = jnp.zeros_like(sums_ref)

    def step(rows):
        given = given_of(rows)
        held = normal[rows, :].astype(F32)
        grad = norm_back(given, held, inverse[rows, :], gain[...])
        low = grad.astype(LOW)
        grad_ref[rows, :] = grad
        low_ref[rows, :] = low
        sums_ref[0:1, :] += jnp.sum(given * held, axis=0, keepdims=True)
        sums_ref[1:2, :] += jnp.sum(given, axis=0, keepdims=True)
        sums_ref[2:3, :] += jnp.sum(low.astype(F32), axis=0, keepdims=True)

    each_tile(normal.shape[0], min(NORM_TILE, size), step)


def norm_two_back_kernel(scalars, ins, *refs):
    section, place = scalars
    upstream, normal, inverse, gain = ins
    if len(upstream) > 1:
        given_ref, *refs = refs
    else:
        *refs, tokens_ref = refs
        unpack(upstream[0], place[0], tokens_ref)
    grad_ref, low_ref, half_ref, sums_ref = refs

    def given_of(rows):
        if len(upstream) == 1:
            return tokens_ref[rows, :].astype(F32)
        given = upstream[0][rows, :] + (upstream[1][rows, :].astype(F32) + upstream[2][rows, :].astype(F32))
        given_ref[rows, :] = given
        return given

    norm_back_tiles(given_of, normal, inverse, gain, grad_ref, low_ref, sums_ref)
    keep_half(low_ref, section[0], half_ref)


def feed_back_kernel(layout, scalars, ins, hidden_ref, sums_ref, *part_refs):
    sources, slope, blocks = ins
    ups, downs = layout.named("up"), layout.named("down")
    row_count, col_count, width = len(blocks), len(blocks[0]), layout.width
    sums_ref[...] = jnp.zeros_like(sums_ref)
    begin = 0
    for source, part_ref in zip(sources, part_refs):
        count = source.shape[0]

        def through(rows, source=source, begin=begin):
            held = source[rows, :]
            here = pl.ds(begin + rows.start, rows.size)
            for j in range(col_count):
                terms = []
                for i in range(row_count):
                    for slab in downs:
                        start = (i * len(downs) + slab.number) * width
                        terms.append(dot_nt(held[:, start : start + width], take_slab(blocks[i][j], slab)))
                result = add_up(terms)
                span = slice(j * result.shape[1], (j + 1) * result.shape[1])
                grad = (result * slope[here, span].astype(F32)).astype(LOW)
                hidden_ref[here, span] = grad
                sums_ref[0:1, span] += jnp.sum(grad.astype(F32), axis=0, keepdims=True)

        each_tile(count, TILE, through)

        def back(rows, begin=begin, part_ref=part_ref):
            held = hidden_ref[pl.ds(begin + rows.start, rows.size), :]
            for i in range(row_count):
                terms = []
                for j in range(col_count):
                    for slab in ups:
                        start = (j * len(ups) + slab.number) * width
                        terms.append(dot_nt(held[:, start : start + width], take_slab(blocks[i][j], slab)))
                result = add_up(terms)
                part_ref[rows, i * result.shape[1] : (i + 1) * result.shape[1]] = result.astype(LOW)

        each_tile(count, TILE, back)
        begin += count


def attend_back_kernel(
    layout, scalars, ins, grad_ref, low_ref, packed_ref, part_ref, sums_ref, bias_sums_ref, context_ref
):
    (section,) = scalars
    above, own, came, mine, others, normal, inverse, gain, queries, keys, values, probs, blocks = ins
    slots, half = queries.shape
    row_count, col_count, width = len(blocks), len(blocks[0]), layout.width

    def given_of(rows):
        return above[rows, :] + branch_tile(rows, own, came, mine, others, section[0])

    norm_back_tiles(given_of, normal, inverse, gain, grad_ref, low_ref, sums_ref, mine.shape[0])

    def to_context(rows):
        held = low_ref[rows, :]
        slabs = layout.named("out")
        for j in range(col_count):
            terms = []
            for i in range(row_count):
                for slab in slabs:
                    start = (i * len(slabs) + slab.number) * width
                    terms.append(dot_nt(held[:, start : start + width], take_slab(blocks[i][j], slab)))
            result = add_up(terms)
            context_ref[rows, j * result.shape[1] : (j + 1) * result.shape[1]] = result.astype(LOW)

    each_tile(slots, TILE, to_context)
    factor = HD ** (-0.5)

    def heads(pair, carry):
        lanes = pl.ds(pl.multiple_of(pair * PAIR, PAIR), PAIR)
        query, key, value = queries[:, lanes], keys[:, lanes], values[:, lanes]
        grad = context_ref[:, lanes]
        grad_heads, key_heads = both_heads(grad), both_heads(key)
        grad_turned, query_turned = grad.T, query.T
        grad_queries, grad_keys, grad_values = [], [], []
        for h in range(2):
            span = slice(h * HD, (h + 1) * HD)
            tiles = []
            for start in range(0, slots, TILE):
                rows = slice(start, start + TILE)
                soft_low = probs[2 * pair + h, rows, :]
                soft = soft_low.astype(F32)
                grad_soft = dot_nt(grad_heads[h][rows], value)
                centered = jnp.sum(soft * grad_soft, axis=1, keepdims=True)
                grad_scores = (soft * (grad_soft - centered)).astype(LOW)
                tiles.append(
                    (
                        dot(grad_scores, key_heads[h]),
                        dot(query_turned[span, rows], grad_scores),
                        dot(grad_turned[span, rows], soft_low),
                    )
                )
            grad_queries.append(jnp.concatenate([tile[0] for tile in tiles], axis=0))
            grad_keys.append(add_up([tile[1] for tile in tiles]))
            grad_values.append(add_up([tile[2] for tile in tiles]))
        grad_query = (add_up(grad_queries) * factor).astype(LOW)
        grad_key = (jnp.concatenate(grad_keys, axis=0) * factor).T.astype(LOW)
        grad_value = jnp.concatenate(grad_values, axis=0).T.astype(LOW)
        for n, result in enumerate((grad_query, grad_key, grad_value)):
            packed_ref[:, pl.ds(pl.multiple_of(n * half + pair * PAIR, PAIR), PAIR)] = result
        for n, result in ((0, grad_query), (1, grad_value)):
            bias_sums_ref[n : n + 1, lanes] = jnp.sum(result.astype(F32), axis=0, keepdims=True)
        return carry

    lax.fori_loop(0, half // PAIR, heads, 0, unroll=True)

    def back(rows):
        held = packed_ref[rows, :]
        for i in range(row_count):
            terms = []
            for j in range(col_count):
                for n, name in enumerate(("query", "key", "value")):
                    for slab in layout.named(name):
                        start = n * half + j * (half // col_count) + slab.number * width
                        terms.append(dot_nt(held[:, start : start + width], take_slab(blocks[i][j], slab)))
            result = add_up(terms)
            part_ref[rows, i * result.shape[1] : (i + 1) * result.shape[1]] = result.astype(LOW)

    each_tile(slots, TILE, back)


def all_tokens(segments, lanes):
    if len(segments) == 1:
        return segments[0][:, lanes]
    return jnp.concatenate([segment[:, lanes] for segment in segments], axis=0)


def weight_kernel(layout, grid, plan, axis, scalars, ins, *refs):
    row_count, col_count = grid

    def store(slab, i, j, tile, value):
        value = value.astype(LOW)
        rows = pl.ds(slab.start + tile, value.shape[0])
        if axis is None:
            refs[0][i, j, rows, :] = value
        elif axis == "rows":
            lower = slab.start // (layout.height // 2)
            rows = pl.ds(slab.start % (layout.height // 2) + tile, value.shape[0])
            refs[i][lower, rows, :] = value
        else:
            height = layout.height // len(axis)
            chunk = slab.start // height
            away, other = (i, j) if axis[chunk] == "row" else (j, i)
            refs[2 * chunk + away][other, pl.ds(slab.start % height + tile, value.shape[0]), :] = value

    if len(ins) > 4:
        for ref in refs[:2]:
            for b in range(ref.shape[0]):
                ref[b, layout.height // len(axis) :, :] = ins[4][...]
    done = []
    for slab in layout.slabs:
        left, right, right_start, left_by_row = plan[slab.name]
        if (left, left_by_row) in done:
            continue
        done.append((left, left_by_row))
        sharing = [s for s in layout.slabs if plan[s.name][0] == left and plan[s.name][3] == left_by_row]
        height = slab.height
        tile = min(TILE, height)
        outer, inner = (row_count, col_count) if left_by_row else (col_count, row_count)
        for a in range(outer):

            def step(number, carry, a=a, sharing=sharing, tile=tile, height=height, left=left):
                start = pl.multiple_of(number * tile, tile)
                turned = all_tokens(ins[left], pl.ds(pl.multiple_of(a * height + start, tile), tile)).T
                for s in sharing:
                    _, right, right_start, by_row = plan[s.name]
                    count = sum(t.name == s.name for t in layout.slabs)
                    for b in range(inner):
                        column = right_start + (b * count + s.number) * layout.width
                        value = dot(turned, all_tokens(ins[right], slice(column, column + layout.width)))
                        i, j = (a, b) if by_row else (b, a)
                        store(s, i, j, start, value)
                return carry

            lax.fori_loop(0, height // tile, step, 0, unroll=True)


def collect_kernel(scalars, ins, stored_ref, total_ref):
    section, place = scalars
    first, own, came, second = ins

    @pl.when(section[0] == 0)
    def _():
        def step(rows):
            total_ref[rows, :] = first[rows, :] + (own[rows, :].astype(F32) + came[rows, :].astype(F32))

        each_tile(first.shape[0], NORM_TILE, step)
        pack(total_ref, place[0], stored_ref)

    @pl.when(section[0] != 0)
    def _():
        pack(second, place[0], stored_ref)


def attend_forward(inputs, lengths, place, layout, attn, small):
    half, width = small["query_bias"].shape[1], small["out_bias"].shape[1]
    tokens = inputs.shape[0] if inputs.ndim == 2 else 2 * inputs.shape[1]
    low = lambda n: shaped((tokens, n), LOW)
    results = launch(
        functools.partial(attend_kernel, layout),
        ((low(width),) if inputs.ndim == 3 else ())
        + (low(half), low(half), low(half), shaped((half // HD, tokens, tokens), LOW), low(half), low(width)),
        (inputs, small["query_bias"], small["value_bias"], attn),
        flops=8 * tokens * width * half + 16 * tokens * tokens * half,
        scalars=(lengths, place),
    )
    return results if inputs.ndim == 3 else [inputs, *results]


def norm_forward(inputs, own, came, section_at, small):
    tokens, width = inputs.shape
    low, high = (lambda n: shaped((tokens, n), LOW)), (lambda n: shaped((tokens, n), F32))
    return launch(
        norm_kernel,
        (high(width), low(width), shaped((tokens // 2, width), LOW), low(width), high(1)),
        (inputs, own, came, small["out_bias"], small["norm1_gain"], small["norm1_shift"]),
        scalars=(section_at,),
    )


def feed_forward(sources, layout, feed, small):
    width, hidden = sources[0].shape[1], small["up_bias"].shape[1]
    tokens = sum(source.shape[0] for source in sources)
    parts = tuple(shaped(source.shape, LOW) for source in sources)
    return launch(
        functools.partial(feed_kernel, layout),
        (shaped((tokens, hidden), LOW), shaped((tokens, hidden), LOW), *parts),
        (sources, small["up_bias"], feed),
        flops=4 * tokens * width * hidden,
    )


def finish_forward(normed, own, came, mine, others, section_at, place, small):
    tokens, width = normed.shape
    grid = lax.axis_size("row") * lax.axis_size("col")
    low = lambda n: shaped((tokens, n), LOW)
    return launch(
        finish_kernel,
        (low(width), shaped((grid, tokens // 4, 2 * width // grid), LOW), low(width), shaped((tokens, 1), F32)),
        (normed, own, came, mine, others, small["down_bias"], small["norm2_gain"], small["norm2_shift"]),
        scalars=(section_at, place),
    )


def weight_grads(layout, plan, operands, tokens, axis):
    row_count, col_count = lax.axis_size("row"), lax.axis_size("col")
    height, width = layout.height, layout.width
    if axis == "rows":
        col_count = 1
        outputs = (shaped((2, height // 2, width), LOW),) * row_count
    elif small_grid():
        extra = [operands[4].shape[0], *[0] * (len(axis) - 1)]
        outputs = [shaped((2, height // len(axis) + more, width), LOW) for more in extra for _ in range(2)]
    else:
        axis = None
        outputs = (shaped((row_count, col_count, height, width), LOW),)
    return launch(
        functools.partial(weight_kernel, layout, (row_count, col_count), plan, axis),
        outputs,
        operands,
        flops=2 * tokens * height * width * row_count * col_count,
    )


def norm_two_back(upstream, normal, inverse, section_at, place, small):
    tokens, width = normal.shape
    low, high = (lambda n: shaped((tokens, n), LOW)), (lambda n: shaped((tokens, n), F32))
    given = (high(width),) if len(upstream) > 1 else ()
    *given, grad, branch_low, half_low, sums = launch(
        norm_two_back_kernel,
        (*given, high(width), low(width), shaped((tokens // 2, width), LOW), shaped((8, width), F32)),
        (upstream, normal, inverse, small["norm2_gain"]),
        scratch=() if given else (pltpu.VMEM((tokens, width), LOW),),
        scalars=(section_at, place),
    )
    return given, grad, branch_low, half_low, sums


def feed_back(sources, slope, layout, feed):
    tokens, hidden = slope.shape
    width = sources[0].shape[1]
    parts = tuple(shaped(source.shape, LOW) for source in sources)
    return launch(
        functools.partial(feed_back_kernel, layout),
        (shaped((tokens, hidden), LOW), shaped((8, hidden), F32), *parts),
        (sources, slope, feed),
        flops=4 * tokens * width * hidden,
    )


def attend_back(above, parts, normal, inverse, queries, keys, values, probs, section_at, layout, attn, small):
    tokens, width = normal.shape
    half = queries.shape[1]
    low, high = (lambda n: shaped((tokens, n), LOW)), (lambda n: shaped((tokens, n), F32))
    grad, attended_low, packed, own, sums, bias_sums = launch(
        functools.partial(attend_back_kernel, layout),
        (high(width), low(width), low(3 * half), low(width), shaped((8, width), F32), shaped((8, half), F32)),
        (above, *parts, normal, inverse, small["norm1_gain"], queries, keys, values, probs, attn),
        scratch=[pltpu.VMEM((tokens, half), LOW)],
        flops=8 * tokens * width * half + 32 * tokens * tokens * half,
        scalars=(section_at,),
    )
    grads = {"norm1_gain": sums[0], "norm1_shift": sums[1], "out_bias": sums[2]}
    grads |= {"query_bias": bias_sums[0], "value_bias": bias_sums[1]}
    return grad, attended_low, packed, own, grads


FEED_PLAN = {"up": (0, 1, 0, True), "down": (2, 3, 0, False)}


def attn_plan(half):
    return {
        "query": (0, 1, 0, True),
        "key": (0, 1, half, True),
        "value": (0, 1, 2 * half, True),
        "out": (2, 3, 0, False),
    }


HALVED = ("query_bias", "value_bias", "up_bias")
WHOLE = ("out_bias", "norm1_gain", "norm1_shift", "down_bias", "norm2_gain", "norm2_shift")


def body(
    tokens_in,
    lengths,
    placement,
    cotangent,
    qkv_weight,
    qv_bias,
    out_weight,
    out_bias,
    norm1_gain,
    norm1_shift,
    up_weight,
    up_bias,
    down_weight,
    down_bias,
    norm2_gain,
    norm2_shift,
):
    row_count, col_count = lax.axis_size("row"), lax.axis_size("col")
    grid = row_count * col_count
    section, group = lax.axis_index("section"), lax.axis_index("dp")
    row, col = lax.axis_index("row"), lax.axis_index("col")
    is_first = section == 0
    seq_local, half_slots, _, packed_width = tokens_in.shape
    if seq_local != grid or col_count != 2 or lax.axis_size("dp") != 4:
        raise ValueError("unexpected grid")
    features = packed_width // 2
    seq_total = placement.shape[0]
    width = features * grid
    section_at, place = section.reshape(1), row.reshape(1)

    attn_layout = make_layout(
        [(name, qkv_weight.shape[2], qkv_weight.shape[3] // 2) for name in ("query", "key", "value")]
        + [("out", out_weight.shape[1] // 2, out_weight.shape[2])]
    )
    feed_layout = make_layout(
        [("up", up_weight.shape[1], up_weight.shape[2] // 2), ("down", down_weight.shape[1] // 2, down_weight.shape[2])]
    )

    def exchange(stored):
        return lax.all_to_all(stored, ("row", "col"), split_axis=0, concat_axis=0, tiled=True)

    def both_layers(layout, operands, sources):
        piece = shaped((layout.height, layout.width), LOW)
        stays, leaves = launch(
            functools.partial(halves_kernel, layout, sources), (piece, piece), operands, scalars=(section_at,)
        )
        came = swap_section(leaves)
        return jnp.where(is_first, stays, came), jnp.where(is_first, came, stays)

    attn_pieces = both_layers(
        attn_layout,
        (qkv_weight[0], out_weight[0]),
        {
            "query": (lambda ins: ins[0].at[0], False),
            "key": (lambda ins: ins[0].at[1], False),
            "value": (lambda ins: ins[0].at[2], False),
            "out": (lambda ins: ins[1], True),
        },
    )
    attn_near = gather_first(attn_pieces[0])
    inputs = exchange(tokens_in[:, :, 0])
    attn_near = after(attn_near, inputs)
    feed_pieces = both_layers(
        feed_layout,
        (after(up_weight[0], attn_pieces), down_weight[0]),
        {"up": (lambda ins: ins[0], False), "down": (lambda ins: ins[1], True)},
    )
    small_own = (qv_bias, up_bias, out_bias, norm1_gain, norm1_shift, down_bias, norm2_gain, norm2_shift)
    sizes = [t.size for t in small_own]
    flat = jnp.concatenate([t.reshape(-1) for t in small_own])
    padded = -(-flat.size // 2048) * 2048
    flat = jnp.pad(flat, (0, padded - flat.size)).reshape(-1, 128)
    flat_near = gather_first(flat)
    flat_blocks = gather_second(flat, flat_near, "row")
    flat_own = jnp.stack([jnp.stack([jnp.concatenate(b).reshape(-1) for b in line]) for line in flat_blocks])
    flat_own = jnp.roll(flat_own, col, axis=1)
    flat_other = swap_section(flat_own.reshape(-1, 128)).reshape(flat_own.shape)
    flat_all = [jnp.where(is_first, flat_own, flat_other), jnp.where(is_first, flat_other, flat_own)]
    starts = [sum(sizes[:n]) for n in range(len(sizes) + 1)]

    def own_part(by_col, count, which):
        halves = by_col.reshape(*by_col.shape[:-1], count, -1)
        chosen = lax.dynamic_index_in_dim(halves, which, axis=halves.ndim - 2, keepdims=False)
        return jnp.roll(chosen, -col, axis=-2) if chosen.shape[-2] > 1 else chosen

    smalls = []
    for layer in range(2):
        fields = [flat_all[layer][..., starts[n] : starts[n + 1]] for n in range(len(sizes))]
        rows_first = [jnp.roll(field, row, axis=0) for field in fields[:2]]
        qv = rows_first[0].reshape(row_count, col_count, 2, -1).transpose(2, 1, 0, 3)
        qv = own_part(qv.reshape(2, col_count, -1), 2, section).reshape(2, -1)
        up_shift = rows_first[1].transpose(1, 0, 2).reshape(col_count, -1)
        up_shift = lax.dynamic_index_in_dim(up_shift, col, axis=0)
        up_shift = own_part(up_shift, 2, section).reshape(1, -1)
        small = {"query_bias": qv[:1], "value_bias": qv[1:], "up_bias": up_shift}
        for name, field in zip(WHOLE, fields[2:]):
            small[name] = field.reshape(1, -1)
        smalls.append(small)

    own_lengths = lax.dynamic_slice_in_dim(lengths, group * seq_local + row * col_count + col, 1)

    cot_all = lax.all_gather(cotangent[:, :, 0], "dp", axis=0, tiled=True)
    wanted = group * seq_local + lax.broadcasted_iota(jnp.int32, (seq_local,), 0)
    matches = placement[None, :] == wanted[:, None]
    position = jnp.sum(
        jnp.where(matches, lax.broadcasted_iota(jnp.int32, (seq_local, seq_total), 1), 0), axis=1
    )
    cot_held = jnp.take(cot_all, position, axis=0)

    attn_first = gather_second(attn_pieces[0], attn_near, "col")
    feed_first = gather_rows(after(feed_pieces[0], attn_near, flat_blocks))
    small = smalls[0]
    def to_dealt(stored):
        held = lax.all_gather(exchange(stored), "dp", axis=0, tiled=True)
        return jnp.take(held, lax.dynamic_slice_in_dim(placement, group * seq_local, seq_local), axis=0)

    near = after(attn_pieces[1], attn_first)
    near = fetch(near, "col", 1) if small_grid() else gather_first(near)
    inputs, *attended_first, own = attend_forward(inputs, own_lengths, place, attn_layout, attn_first, small)
    came = swap_section(own)
    normed, low, half_low, *normed_first = norm_forward(inputs, own, came, section_at, small)
    got = pair_col(half_low)
    feed_first = after(feed_first, half_low)
    active, slope, own = feed_forward([low], feed_layout, feed_first, small)
    came = swap_section(own)
    pair_low = both_halves(got, own, near)
    far = fetch(after(attn_pieces[1], feed_first), "row", 1) if small_grid() else near
    pair_active, pair_slope, mine, others = feed_forward(pair_low, feed_layout, feed_first, small)
    fed_first = ([low, *pair_low], [active, pair_active], (slope, pair_slope))
    mine, others = both_halves(to_pair(mine, others), far)
    attn_second = gather_second(attn_pieces[1], after((far, near), own) if small_grid() else near, "row")
    feed_second = gather_rows(after(feed_pieces[1], attn_second))
    middle, first_stored, *finished_first = finish_forward(normed, own, came, mine, others, section_at, place, small)
    small = smalls[1]
    first_dealt = to_dealt(first_stored)
    _, *attended_second, own = attend_forward(middle, own_lengths, place, attn_layout, attn_second, small)
    came = swap_section(own)
    normed, low, half_low, *normed_second = norm_forward(middle, own, came, section_at, small)
    got = pair_col(half_low)
    feed_second = after(feed_second, half_low)
    active, slope, own = feed_forward([low], feed_layout, feed_second, small)
    came = swap_section(own)
    pair_low = both_halves(got, own)
    upstream = exchange(after(cot_held, pair_low))
    pair_active, pair_slope, mine, others = feed_forward(pair_low, feed_layout, feed_second, small)
    fed_second = ([low, *pair_low], [active, pair_active], (slope, pair_slope))
    mine, others = both_halves(to_pair(mine, others))
    _, second_stored, *finished_second = finish_forward(normed, own, came, mine, others, section_at, place, small)

    def small_rows(grads):
        up = grads["up_bias"].reshape(1, -1)
        up = jnp.concatenate([up, *[jnp.zeros_like(up)] * (col_count - 1)])
        grads = grads | {"up_bias": up}
        parts = [jnp.roll(grads[name].reshape(col_count, -1), col, axis=0).reshape(-1) for name in HALVED]
        parts += [jnp.roll(grads[name].reshape(row_count, -1), row, axis=0).reshape(-1) for name in WHOLE]
        vector = jnp.concatenate(parts)
        lanes = attn_layout.width
        count = -(-vector.size // (16 * lanes)) * 16
        return jnp.pad(vector, (0, count * lanes - vector.size)).reshape(count, lanes)

    axes = ("row", "col")

    def attn_grads(source, attended, attended_low, packed, small):
        operands = ([source], [packed], [attended[4]], [attended_low])
        small = small_rows(small)
        if small_grid():
            operands = (*operands, small.astype(LOW))
        parts = weight_grads(attn_layout, attn_plan(width // 2), operands, 2 * half_slots, axes)
        return ([parts[:2], parts[2:]] if small_grid() else [parts]), small

    def all_first(parts):
        return [scatter_first(part, axis) for part, axis in zip(parts, axes)]

    def all_middle(parts, moved):
        return [scatter_middle(*both) for both in zip(parts, moved)]

    def all_second(middles):
        return [scatter_second(middle, axis) for middle, axis in zip(middles, axes)]

    def all_last(parts, middles, seconds, small):
        totals = [scatter_last(*each) for each in zip(parts, middles, seconds)]
        if small_grid():
            return totals
        return [jnp.concatenate([*totals, lax.psum(small, ("row", "col")).astype(LOW)])]

    def all_add(totals, came):
        return [add_low(*both) for both in zip(totals, came)]

    def feed_weights(fed, branches, hiddens):
        lows, actives, _ = fed
        return weight_grads(feed_layout, FEED_PLAN, (lows, hiddens, actives, branches), 4 * half_slots, "rows")

    small = smalls[1]
    _, grad, branch_low, half_low, sums = norm_two_back(
        (upstream,), *finished_second, section_at, place, small
    )
    got = pair_col(half_low)
    hidden, hidden_sums, own = feed_back([branch_low], fed_second[2][0], feed_layout, feed_second)
    came = swap_section(own)
    pair_low = both_halves(got, own)
    second_dealt = to_dealt(after(second_stored, pair_low, first_dealt))
    pair_hidden, pair_sums, mine, others = feed_back(pair_low, fed_second[2][1], feed_layout, feed_second)
    got = to_pair(mine, others)
    small_grads = {"norm2_gain": sums[0], "norm2_shift": sums[1], "down_bias": sums[2]}
    small_grads["up_bias"] = hidden_sums[0] + pair_sums[0]
    parts_second = feed_weights(fed_second, [branch_low, *pair_low], [hidden, pair_hidden])
    mine, others = both_halves(got, parts_second)
    came_second = rows_sent(parts_second)
    grad, attended_low, packed, own, more = attend_back(
        grad, (own, came, mine, others), *normed_second, *attended_second[:4], section_at, attn_layout, attn_second, small
    )
    came = swap_section(own)
    small_second = small_grads | more
    small = smalls[0]
    given, grad, branch_low, half_low, sums = norm_two_back(
        (grad, own, came), *finished_first, section_at, place, small
    )
    got = pair_col(half_low)
    attn_parts_second, rows_second = attn_grads(
        middle, attended_second, after(attended_low, half_low), packed, small_second
    )
    came_second = after(came_second, attn_parts_second)
    feed_second = rows_sum(parts_second, came_second)
    feed_in = group_in(feed_second)
    attn_moved_second = all_first(after(attn_parts_second, feed_second))
    branch_low = after(branch_low, feed_second)
    hidden, hidden_sums, own = feed_back([branch_low], fed_first[2][0], feed_layout, feed_first)
    came = swap_section(own)
    pair_low = both_halves(got, own)
    pair_hidden, pair_sums, mine, others = feed_back(pair_low, fed_first[2][1], feed_layout, feed_first)
    got = to_pair(mine, others)
    attn_middle_second = all_middle(attn_parts_second, after(attn_moved_second, pair_hidden))
    attn_far_second = all_second(attn_middle_second)
    small_grads = {"norm2_gain": sums[0], "norm2_shift": sums[1], "down_bias": sums[2]}
    small_grads["up_bias"] = hidden_sums[0] + pair_sums[0]
    parts_first = feed_weights(fed_first, [branch_low, *pair_low], [hidden, after(pair_hidden, attn_middle_second)])
    came_first = rows_sent(parts_first)
    feed_second = add_low(feed_second, after(feed_in, parts_first))
    feed_across = group_across(feed_second)
    mine, others = both_halves(got, parts_first)
    attn_second = all_last(attn_parts_second, attn_middle_second, after(attn_far_second, parts_first), rows_second)
    attn_second = jnp.concatenate(attn_second)
    attn_in = group_in(attn_second)
    mine = after(mine, feed_second, attn_second, second_dealt)
    grad, attended_low, packed, own, more = attend_back(
        grad, (own, came, mine, others), *normed_first, *attended_first[:4], section_at, attn_layout, attn_first, small
    )
    came = swap_section(own)
    small_first = small_grads | more

    in_middle = (group == 1) | (group == 2)

    def settled(total, outward):
        return jnp.where(in_middle, total, outward)

    def all_settled(totals, outwards):
        return [settled(*both) for both in zip(totals, outwards)]

    attn_second = add_low(attn_second, after(attn_in, own))
    attn_across = group_across(attn_second)
    attn_parts_first, rows_first = attn_grads(
        inputs, attended_first, after(attended_low, attn_second), packed, small_first
    )
    attn_moved_first = all_first(attn_parts_first)
    (stored_grad,) = launch(
        collect_kernel,
        (shaped((grid, half_slots, packed_width), F32),),
        (after(grad, attn_parts_first), own, came, *given),
        scratch=[pltpu.VMEM((2 * half_slots, width), F32)],
        scalars=(section_at, place),
    )
    came_first = after(came_first, stored_grad)
    up_first, down_first = (rows_sum([part[half] for part in parts_first], [part[half] for part in came_first]) for half in range(2))
    up_in, down_in = group_in(up_first), group_in(down_first)
    feed_second = add_low(feed_second, after(feed_across, up_first, down_first))
    feed_out = group_out(feed_second)
    attn_second = add_low(attn_second, after(attn_across, feed_second))
    attn_out = group_out(attn_second)
    attn_middle_first = all_middle(attn_parts_first, after(attn_moved_first, attn_second))
    attn_far_first = all_second(attn_middle_first)
    up_first = add_low(up_first, after(up_in, attn_middle_first))
    up_across = group_across(up_first)
    attn_first = all_last(attn_parts_first, attn_middle_first, after(attn_far_first, up_first), rows_first)
    last_in = [group_in(part) for part in attn_first]
    down_first = add_low(down_first, after(down_in, attn_first))
    down_across = group_across(down_first)
    feed_second = settled(feed_second, after(feed_out, down_first))
    up_first = add_low(up_first, after(up_across, feed_second))
    up_out_first = group_out(up_first)
    input_grad = exchange(after(stored_grad, attn_first))
    attn_first = all_add(attn_first, after(last_in, up_first))
    last_across = [group_across(part) for part in attn_first]

    first_dealt, second_dealt = after((first_dealt, second_dealt), attn_first)
    own_half = jnp.where(is_first, first_dealt, second_dealt)
    other_half = swap_section(jnp.where(is_first, second_dealt, first_dealt))
    layer_out = jnp.concatenate(
        [jnp.where(is_first, own_half, other_half), jnp.where(is_first, other_half, own_half)], axis=1
    )
    down_first = add_low(down_first, after(down_across, attn_first))
    down_out_first = group_out(down_first)
    attn_second = settled(attn_second, after(attn_out, down_first, layer_out, input_grad))
    up_first = settled(up_first, after(up_out_first, attn_second))
    attn_first = all_add(attn_first, after(last_across, up_first))
    last_out = [group_out(part) for part in attn_first]
    down_first = settled(down_first, after(down_out_first, last_out[0]))

    feed_first = [up_first, down_first]
    if small_grid():
        held = attn_layout.height // 2
        extra = attn_second.shape[0] - 2 * held
        attn_second = [attn_second[: held + extra], attn_second[held + extra :]]
    else:
        attn_second = [attn_second]

    def to_section(first, second):
        return jnp.where(is_first, first, second), swap_section(jnp.where(is_first, second, first))

    feed_stays, feed_came = zip(*[to_section(a, b) for a, b in zip(feed_first, feed_second)])
    up_grad, down_grad = launch(
        functools.partial(
            whole_kernel, feed_layout, {"up": (lambda refs: refs[0], False), "down": (lambda refs: refs[1], True)}
        ),
        (shaped(up_weight.shape[1:], F32), shaped(down_weight.shape[1:], F32)),
        (feed_stays, feed_came),
        scalars=(section_at,),
    )
    attn_first = all_settled(attn_first, after(last_out, up_grad, down_grad))
    attn_stays, attn_came = zip(*[to_section(a, b) for a, b in zip(attn_first, attn_second)])

    qkv_grad, out_grad = launch(
        functools.partial(
            whole_kernel,
            attn_layout,
            {
                "query": (lambda refs: refs[0].at[0], False),
                "key": (lambda refs: refs[0].at[1], False),
                "value": (lambda refs: refs[0].at[2], False),
                "out": (lambda refs: refs[1], True),
            },
        ),
        (shaped(qkv_weight.shape[1:], F32), shaped(out_weight.shape[1:], F32)),
        (attn_stays, attn_came),
        scalars=(section_at,),
    )

    lasting = 2 * (width // 2) + up_bias.size * grid // 2 + len(WHOLE) * width
    held = attn_layout.height // len(attn_first)
    small_stays, small_came = (t[0][held:].reshape(-1)[:lasting].astype(F32) for t in (attn_stays, attn_came))
    small_halves = jnp.stack(
        [jnp.where(is_first, small_stays, small_came), jnp.where(is_first, small_came, small_stays)]
    )
    model, hidden = width // 2, up_bias.size * grid // 2
    ends = (0, model, 2 * model, 2 * model + hidden)

    def own_col_row(begin, end):
        blocks = small_halves[:, begin:end].reshape(2, col_count, -1).transpose(1, 0, 2)
        blocks = blocks.reshape(col_count * row_count, -1)
        return lax.dynamic_index_in_dim(blocks, col * row_count + row, axis=0, keepdims=False)

    query_sum, value_sum, up_sum = (own_col_row(ends[n], ends[n + 1]) for n in range(3))
    qv_grad = jnp.stack([query_sum, value_sum]).reshape(qv_bias.shape)
    up_bias_grad = up_sum.reshape(up_bias.shape)
    rest = small_halves[0, ends[3] :].reshape(len(WHOLE), grid, features)
    rest = lax.dynamic_index_in_dim(rest, row * col_count + col, axis=1, keepdims=False)
    whole_grads = {name: rest[n][None] for n, name in enumerate(WHOLE)}
    return (
        layer_out[None, :, :, None],
        input_grad[None, :, :, None],
        qkv_grad[None],
        qv_grad,
        out_grad[None],
        whole_grads["out_bias"],
        whole_grads["norm1_gain"],
        whole_grads["norm1_shift"],
        up_grad[None],
        up_bias_grad,
        down_grad[None],
        whole_grads["down_bias"],
        whole_grads["norm2_gain"],
        whole_grads["norm2_shift"],
    )


def solution(mesh):
    tokens = P("dp", None, ("row", "col"), None)
    feature = P("section", ("row", "col"))
    outward = P("section", "col", "row")
    hidden = P("section", "col", "row", None)
    qv = P("section", None, "col", "row", None)
    stored = P("section", "dp", None, ("row", "col"), None)
    inward = P("section", "row", "col")
    qkv = P("section", None, "row", "col")
    params = (
        qkv, qv, outward, feature, feature, feature, inward, hidden, outward, feature, feature, feature,
    )
    return jax.shard_map(
        body,
        mesh=mesh,
        in_specs=(tokens, P(), P(), tokens, *params),
        out_specs=(stored, stored, *params),
        check_vma=False,
    )
```
